256 devices in a mesh: facet: 64 (over z_lo, y, x, core), freq: 4 (over z_hi).
Axes of the slice: x: 4, y: 4, z: 8 (z_hi: 4, z_lo: 2; z = z_hi * 2 + z_lo), core: 2. Of those that a mesh axis runs over, the one named last changes fastest.
Arguments:
- visibility: bfloat16 [4, 2, 32768], P('freq', None, 'facet'), may hold values from -6 to 6
- row_target: int32 [4, 32768, 1], P('freq', 'facet'), may hold values from 0 to 63; in each aligned block of 512 rows (0 to 511, 512 to 1023, ..., all dimensions but the last counted through in order) at most 16 rows name the same one
- row_cell: int32 [4, 32768], P('freq', 'facet'), may hold values from 0 to 65535
- row_plane: int32 [4, 32768], P('freq', 'facet'), may hold values from 0 to 7
- kernel_table: bfloat16 [2, 2048, 256], replicated, may hold values from -3 to 3
- subgrid_anchor: int32 [64, 2], P('facet'), may hold values from 0 to 65535
Outputs:
- facet_image: float32 [65536, 128], P(('facet', 'freq'))
The draws below stay inside these ranges and needn't reach their ends.
Inputs may be any that keep to these rules, and one draw needn't show every extreme that they name: `row_target`: among the rows of one device, at most 16 name any one subgrid.
All inputs are finite; a program needn't handle non-finite values.
Results may differ from the reference program's by a relative error of at most 0.006.
Values may be sent and summed in bfloat16 or wider, within the bound.
A program may use at most 128 MiB of HBM per device.

```python
import math
import jax
import jax.numpy as jnp
import numpy as np
from jax import lax

SUB = 256
PLANES = 8
NGRID = 65536
TROWS = 1024
TCOLS = 128
VIS_DEV = 512
ROWS = 32768
CAP = 16
SUBGRIDS = 64
FREQS = 4
N_FACET = 64
N_FREQ = 4


def touch_ends(entries, key, least, top_value):
    place = [jax.random.randint(jax.random.fold_in(key, axis), (), 0, length) for axis, length in enumerate(entries.shape)]
    main_axis = entries.shape.index(max(entries.shape))
    next_to = place[:main_axis] + [(place[main_axis] + 1) % entries.shape[main_axis]] + place[main_axis + 1:]
    return entries.at[tuple(place)].set(least).at[tuple(next_to)].set(top_value)


def block_levels(rng, shape, pieces, smallest, largest):
    gain, own = 1.0, jax.random.fold_in(rng, 6)
    for dim, shards_of in pieces:
        draws = jnp.exp(jax.random.uniform(jax.random.fold_in(own, dim), (shards_of,), jnp.float32, smallest / len(pieces), largest / len(pieces)))
        gain = gain * jnp.repeat(draws, shape[dim] // shards_of).reshape([-1 if axis == dim else 1 for axis in range(len(shape))])
    return gain


def assign_block(own_key, own, number, rows, amount, top, reach, skew):
    order = jax.random.permutation(own_key, amount)
    crowded, ordinary = portions_of(amount, rows * top, reach, skew, True), portions_of(amount, rows * top, reach, skew, False)
    places = jnp.arange(amount)

    def named(tallies, offset_by):
        used = int((tallies > 0).sum())
        fixed = max(1, used // 4)
        passed = fixed + (places - fixed + offset_by * (used - fixed)) % max(1, amount - fixed)
        return jnp.zeros((amount,), jnp.int32).at[order[jnp.where(places < fixed, places, passed)]].set(jnp.asarray(tallies, jnp.int32))

    tallies = jnp.where(number % 4 == 0, named(crowded, number // 4), named(ordinary, number - number // 4 - 1))
    mixed = jax.random.permutation(jax.random.fold_in(own, 3), amount)
    donor, receiver = mixed[0:amount // 2 * 2:2], mixed[1:amount // 2 * 2:2]
    margin = jnp.minimum(tallies[donor] - 1, reach - tallies[receiver]) // 2
    margin = jnp.where((donor == order[0]) | (receiver == order[0]) | (tallies[receiver] == 0), 0, jnp.maximum(margin, 0))
    passed = jax.random.randint(jax.random.fold_in(own, 4), (amount // 2,), 0, 1 << 20) % (margin + 1)
    tallies = tallies.at[donor].add(-passed).at[receiver].add(passed)
    members = jnp.searchsorted(jnp.cumsum(tallies), jnp.arange(rows * top), side="right").astype(jnp.int32)
    listing = members.reshape(top, rows).T
    listing = listing[jax.random.permutation(jax.random.fold_in(own, 1), rows)]
    offset_by = jax.random.randint(jax.random.fold_in(own, 2), (rows, 1), 0, top)
    return jnp.take_along_axis(listing, (jnp.arange(top)[None, :] + offset_by) % top, axis=1)


def portions_of(count, total, limit, skew, full):
    weights = [(1 << 20) // math.isqrt(grade ** skew) + 1 for grade in range(1, count + 1)]
    largest = limit if full else min(limit, max(-(-total // count), total * weights[0] // sum(weights)))
    least = 1 if total - largest >= count - 1 else 0
    holding, spare = [largest] + [least] * (count - 1), total - largest - least * (count - 1)
    while spare > 0:
        free = [i for i in range(1, count) if holding[i] < largest] or [i for i in range(1, count) if holding[i] < limit]
        whole, left = sum([weights[i] for i in free]), spare
        for i in free:
            addition = min(limit - holding[i], max(1, left * weights[i] // whole), spare)
            holding[i] = holding[i] + addition
            spare = spare - addition
    return np.array(holding)


def bell_draw(key, dims, width, limit, shards=(), kind=jnp.bfloat16):
    entries = width * jax.random.normal(key, dims, jnp.float32)
    if shards:
        entries = entries * block_levels(key, dims, shards, -0.22, 0.18)
    return jnp.clip(entries, -limit, limit).astype(kind)


def setup_inputs(seed: int = 0) -> dict:
    streams_of = jax.random.split(jax.random.key(seed), 7)
    visibility = bell_draw(streams_of[0], (FREQS, 2, ROWS), 1.0, 6.0, ((0, 4), (2, 64)))
    row_target_keys = jax.random.split(jax.random.fold_in(streams_of[1], 1), FREQS * ROWS // VIS_DEV)
    row_target_turns = jax.random.permutation(jax.random.fold_in(streams_of[1], 3), FREQS * ROWS // VIS_DEV)
    row_target = jax.vmap(lambda own, number: assign_block(jax.random.fold_in(streams_of[1], 2), own, number, VIS_DEV, SUBGRIDS, 1, CAP, 2))(row_target_keys, row_target_turns).reshape((FREQS, ROWS, 1))
    row_cell = touch_ends(jax.random.randint(streams_of[2], (FREQS, ROWS), 0, SUB * SUB), jax.random.fold_in(streams_of[2], 1), 0, (SUB * SUB) - 1).astype(jnp.int32)
    row_plane = touch_ends(jax.random.randint(streams_of[3], (FREQS, ROWS), 0, PLANES), jax.random.fold_in(streams_of[3], 1), 0, PLANES - 1).astype(jnp.int32)
    kernel_table = bell_draw(streams_of[4], (2, PLANES * SUB, SUB), 0.5, 3.0)
    subgrid_anchor = touch_ends(jax.random.randint(streams_of[5], (SUBGRIDS, 2), 0, NGRID), jax.random.fold_in(streams_of[5], 1), 0, NGRID - 1).astype(jnp.int32)
    return dict(visibility=visibility, row_target=row_target, row_cell=row_cell, row_plane=row_plane, kernel_table=kernel_table, subgrid_anchor=subgrid_anchor)


def phases(spatial, pixel):
    spatial_mod = spatial % NGRID
    pixel_mod = pixel % NGRID
    upper_part = pixel_mod // 256
    lower_part = pixel_mod % 256
    phase_index = (spatial_mod * upper_part % NGRID * 256 + spatial_mod * lower_part) % NGRID
    angles = phase_index.astype(jnp.float32) * (2.0 * math.pi / NGRID)
    return (jnp.cos(angles), jnp.sin(angles))

def grid_slots(values, packed, kernel_table):
    plane_cells = SUB * SUB
    w_plane = packed // plane_cells
    remainder = packed % plane_cells
    u_index = (w_plane * SUB + remainder // SUB).astype(jnp.int32)
    v_index = (w_plane * SUB + remainder % SUB).astype(jnp.int32)
    u_kernel = kernel_table[:, u_index, :]
    v_kernel = kernel_table[:, v_index, :].astype(jnp.float32)
    vis_real = values[0].astype(jnp.float32)[:, None]
    vis_imag = values[1].astype(jnp.float32)[:, None]
    term_real = (vis_real * v_kernel[0] - vis_imag * v_kernel[1]).astype(jnp.bfloat16)
    term_imag = (vis_real * v_kernel[1] + vis_imag * v_kernel[0]).astype(jnp.bfloat16)
    left_rows = jnp.concatenate([u_kernel[0], u_kernel[1]], axis=0)
    right_rows = jnp.concatenate([jnp.concatenate([term_real, term_imag], axis=1), jnp.concatenate([-term_imag, term_real], axis=1)], axis=0)
    return lax.dot_general(left_rows, right_rows, (((0,), (0,)), ((), ())), preferred_element_type=jnp.float32)

def widened_block(block):
    half = block.shape[0]
    return jnp.concatenate([block, jnp.concatenate([-block[:, half:], block[:, :half]], axis=1)], axis=0)

def tile_term(widened, anchor_pair, facet_id, tile_lines, scale):
    spatial_u = anchor_pair[0] + jnp.arange(SUB, dtype=jnp.int32)
    spatial_v = anchor_pair[1] + jnp.arange(SUB, dtype=jnp.int32)
    pixels = facet_id // 8 * (NGRID // 8) + tile_lines
    cos_left, sin_left = phases(spatial_u[None, :], pixels[:, None])
    left_rows = jnp.concatenate([cos_left, sin_left], axis=1).astype(jnp.bfloat16)
    mixed = jnp.dot(left_rows, widened, preferred_element_type=jnp.float32).astype(jnp.bfloat16)
    columns = facet_id % 8 * (NGRID // 8) + jnp.arange(TCOLS, dtype=jnp.int32)
    cos_right, sin_right = phases(spatial_v[:, None], columns[None, :])
    right_rows = jnp.concatenate([cos_right, -sin_right], axis=0).astype(jnp.bfloat16)
    return jnp.dot(mixed, right_rows, preferred_element_type=jnp.float32) * scale

def reference(visibility, row_target, row_cell, row_plane, kernel_table, subgrid_anchor):
    capacity = 2 * VIS_DEV // N_FACET
    slot_count = N_FACET * capacity
    scale = 1.0 / (SUB * math.sqrt(N_FACET * N_FREQ * VIS_DEV))
    summed = jnp.zeros((SUBGRIDS, SUB, 2 * SUB), jnp.float32)

    def grid_member(member):
        return grid_slots(member[0], member[1], kernel_table)
    for band in range(FREQS):
        destination = row_target[band, :, 0].reshape(N_FACET, VIS_DEV)
        onehot = (destination[:, :, None] == jnp.arange(SUBGRIDS, dtype=jnp.int32)[None, None, :]).astype(jnp.int32)
        position = lax.optimization_barrier(jnp.sum(onehot * (jnp.cumsum(onehot, axis=1) - 1), axis=2))
        source = jnp.arange(N_FACET, dtype=jnp.int32)[:, None]
        flat_slot = (destination * slot_count + source * capacity + position).reshape(-1).astype(jnp.int32)
        values = jnp.zeros((2, SUBGRIDS * slot_count), jnp.bfloat16).at[:, flat_slot].set(visibility[band])
        packed = jnp.zeros((SUBGRIDS * slot_count,), jnp.int32).at[flat_slot].set(row_plane[band] * (SUB * SUB) + row_cell[band])
        values = values.reshape(2, SUBGRIDS, slot_count).transpose(1, 0, 2)
        packed = packed.reshape(SUBGRIDS, slot_count)
        summed = summed + lax.map(grid_member, (values, packed))
    blocks = summed.astype(jnp.bfloat16)
    tile_lines = jnp.arange(TROWS, dtype=jnp.int32)

    def facet_tile(facet_id):

        def add_subgrid(carry, member):
            return (carry + tile_term(widened_block(member[0]), member[1], facet_id, tile_lines, scale), None)
        tile, unused = lax.scan(add_subgrid, jnp.zeros((TROWS, TCOLS), jnp.float32), (blocks, subgrid_anchor))
        return tile
    image = lax.map(facet_tile, jnp.arange(N_FACET, dtype=jnp.int32))
    return image.reshape(N_FACET * TROWS, TCOLS)
```

```python
import functools
import math

import jax
import jax.numpy as jnp
from jax import lax
from jax.experimental import pallas as pl
from jax.experimental.pallas import tpu as pltpu
from jax.sharding import PartitionSpec as P

NGRID = 65536
TROWS = 1024
TCOLS = 128
SUB = 256
PLANES = 8
CAP = 16
RADIX = 8
LANES = 128
KS = SUB // RADIX
MESH = pl.DeviceIdType.MESH
F32, BF16, I32 = jnp.float32, jnp.bfloat16, jnp.int32


def turn(index):
    index = index & (NGRID - 1)
    quadrant = (index + NGRID // 8) >> 14
    rest = (index - (quadrant << 14)).astype(F32) * (2.0 * math.pi / NGRID)
    square = rest * rest
    sine = rest * (1.0 + square * (-1.0 / 6 + square * (1.0 / 120 + square * (-1.0 / 5040 + square * (1.0 / 362880)))))
    cosine = 1.0 + square * (-0.5 + square * (1.0 / 24 + square * (-1.0 / 720 + square * (1.0 / 40320))))
    odd = (quadrant & 1) == 1
    c = jnp.where(odd, sine, cosine)
    s = jnp.where(odd, cosine, sine)
    c = jnp.where(((quadrant + 1) & 2) == 2, -c, c)
    s = jnp.where((quadrant & 2) == 2, -s, s)
    return c, s


def iota(shape, dim):
    return lax.broadcasted_iota(I32, shape, dim)


def nt_dot(a, b):
    return lax.dot_general(a, b, (((1,), (1,)), ((), ())), preferred_element_type=F32)


def tn_dot(a, b):
    return lax.dot_general(a, b, (((0,), (0,)), ((), ())), preferred_element_type=F32)


def dot(a, b):
    return jnp.dot(a, b, preferred_element_type=F32)


def kernel(
    facets, bands, scale,
    vis_ref, target_ref, cell_ref, plane_ref, anchor_ref, table_hbm, out_ref,
    table, send1, recv1, right, send2, recv2, left, send3, recv3, send4, recv4,
    table_sem, send_sems, recv_sems,
):
    me = lax.axis_index("facet")
    band = lax.axis_index("freq")
    my_class, my_column = me // RADIX, me % RADIX
    rows = vis_ref.shape[1]
    cells = PLANES * SUB
    band_rows = TROWS // bands

    load_table = pltpu.make_async_copy(table_hbm, table, table_sem)
    load_table.start()

    barrier = pltpu.get_barrier_semaphore()

    @pl.loop(1, facets)
    def _(offset):
        pl.semaphore_signal(
            barrier, inc=1, device_id={"facet": lax.rem(me + offset, facets)}, device_id_type=MESH
        )

    for offset in range(1, bands):
        pl.semaphore_signal(
            barrier, inc=1, device_id={"freq": lax.rem(band + offset, bands)}, device_id_type=MESH
        )

    named = iota((facets, rows), 0) == target_ref[...]
    named_f = jnp.where(named, 1.0, 0.0)
    named_b = named_f.astype(BF16)
    earlier = jnp.where(iota((rows, rows), 0) < iota((rows, rows), 1), 1.0, 0.0).astype(BF16)
    position = jnp.sum(named_f * dot(named_b, earlier), axis=0, keepdims=True)
    here = iota((CAP, rows), 0).astype(F32) == position
    vis = vis_ref[...].astype(F32)
    cell = cell_ref[...]
    payloads = (
        vis[0:1], vis[1:2], (cell >> 8).astype(F32), (cell & 255).astype(F32), plane_ref[...].astype(F32),
    )
    spread = [jnp.where(here, payload, 0.0) for payload in payloads]
    spread.append(jnp.zeros((LANES - CAP * len(payloads), rows), F32))
    slots = nt_dot(named_b, jnp.concatenate(spread, axis=0).astype(BF16))
    lane = iota((facets, LANES), 1)
    us, vs = anchor_ref[0, 0], anchor_ref[0, 1]
    slots = jnp.where(lane == CAP * 5, us.astype(F32), slots)
    send1[...] = slots.reshape(facets, 1, LANES)
    recv1[pl.ds(me, 1)] = send1[pl.ds(me, 1)]

    pl.semaphore_wait(barrier, facets - 1 + bands - 1)

    @pl.loop(1, facets)
    def _(offset):
        peer = lax.rem(me + offset, facets)
        pltpu.make_async_remote_copy(
            src_ref=send1.at[peer], dst_ref=recv1.at[me], send_sem=send_sems.at[0], recv_sem=recv_sems.at[0],
            device_id={"facet": peer}, device_id_type=MESH,
        ).start()

    def settle(source, target, phase, axis, count, amount):
        return pltpu.make_async_remote_copy(
            src_ref=source.at[pl.ds(0, amount)], dst_ref=target.at[pl.ds(0, amount)],
            send_sem=send_sems.at[phase], recv_sem=recv_sems.at[phase],
            device_id={axis: lax.rem(lax.axis_index(axis) + 1, count)}, device_id_type=MESH,
        )

    for group in range(RADIX):
        spatial = vs + iota((SUB, TCOLS), 0)
        pixel = iota((SUB, TCOLS), 1)
        index = (((spatial & (RADIX - 1)) * group & (RADIX - 1)) << 13) + spatial * pixel
        cos_r, sin_r = turn(index)
        cos_r, sin_r = cos_r.astype(BF16), sin_r.astype(BF16)
        right[group, :SUB, :TCOLS] = cos_r
        right[group, :SUB, TCOLS:] = sin_r
        right[group, SUB:, :TCOLS] = -sin_r
        right[group, SUB:, TCOLS:] = cos_r

    load_table.wait()
    wait1 = settle(send1, recv1, 0, "facet", facets, facets - 1)
    wait1.wait_recv()

    got = recv1[...].reshape(facets, LANES)
    u_cell = got[:, 2 * CAP:3 * CAP] + got[:, 4 * CAP:5 * CAP] * SUB
    v_cell = got[:, 3 * CAP:4 * CAP] + got[:, 4 * CAP:5 * CAP] * SUB
    every = iota((facets, cells), 1).astype(F32)

    def picker(values):
        return jnp.concatenate(
            [jnp.where(every == values[:, q:q + 1], 1.0, 0.0).astype(BF16) for q in range(CAP)], axis=0
        )

    pick_u, pick_v = picker(u_cell), picker(v_cell)
    a_real = dot(pick_u, table[0]).astype(BF16)
    a_imag = dot(pick_u, table[1]).astype(BF16)
    k_real = dot(pick_v, table[0])
    k_imag = dot(pick_v, table[1])
    v_real = jnp.concatenate([got[:, q:q + 1] for q in range(CAP)], axis=0)
    v_imag = jnp.concatenate([got[:, CAP + q:CAP + q + 1] for q in range(CAP)], axis=0)
    b_real = (v_real * k_real - v_imag * k_imag).astype(BF16)
    b_imag = (v_real * k_imag + v_imag * k_real).astype(BF16)
    b_wide = jnp.concatenate([b_real, b_imag], axis=1)
    b_turned = jnp.concatenate([-b_imag, b_real], axis=1)
    grid = (tn_dot(a_real, b_wide) + tn_dot(a_imag, b_turned)).astype(BF16)
    place = iota((SUB, SUB), 0)
    wanted = ((place & (KS - 1)) << 3) + (((place >> 5) - us) & (RADIX - 1))
    order = jnp.where(iota((SUB, SUB), 1) == wanted, 1.0, 0.0).astype(BF16)
    grid = dot(order, grid).astype(BF16)

    @pl.loop(0, RADIX)
    def _(step):
        column = lax.rem(my_column + step, RADIX)
        half = dot(grid, right[column]).astype(BF16)
        for c in range(RADIX):
            send2[c * RADIX + column] = half[c * KS:(c + 1) * KS]

        @pl.loop(0, RADIX)
        def _(turn_by):
            peer = lax.rem(my_class + turn_by, RADIX) * RADIX + column

            @pl.when(peer != me)
            def _():
                pltpu.make_async_remote_copy(
                    src_ref=send2.at[peer], dst_ref=recv2.at[me],
                    send_sem=send_sems.at[1], recv_sem=recv_sems.at[1],
                    device_id={"facet": peer}, device_id_type=MESH,
                ).start()

    recv2[pl.ds(me, 1)] = send2[pl.ds(me, 1)]

    width = facets * KS
    own_s = iota((facets, width), 0) == (iota((facets, width), 1) >> 5)
    first = jnp.sum(jnp.where(own_s, got[:, 5 * CAP:5 * CAP + 1], 0.0), axis=0, keepdims=True).astype(I32)
    first = first + ((my_class - first) & (RADIX - 1))
    spatial = first + ((iota((1, width), 1) & (KS - 1)) << 3)
    fine = 32
    coarse_r, coarse_i = turn(iota((TROWS // fine, width), 0) * fine * spatial)
    fine_r, fine_i = turn(iota((fine, width), 0) * spatial)
    for piece in range(TROWS // fine):
        p_r, p_i = coarse_r[piece:piece + 1], coarse_i[piece:piece + 1]
        base = piece * fine
        block = base // band_rows
        at = base % band_rows
        left[block, at:at + fine] = (p_r * fine_r - p_i * fine_i).astype(BF16)
        left[block, band_rows + at:band_rows + at + fine] = (p_r * fine_i + p_i * fine_r).astype(BF16)

    wait2 = settle(send2, recv2, 1, "facet", facets, facets - 1)
    wait2.wait_recv()

    mixed = recv2[...].reshape(width, 2 * TCOLS)

    def tile_part(block):
        both = dot(left[block], mixed)
        upper, lower = both[:band_rows], both[band_rows:]
        return jnp.concatenate(
            [upper[:, :TCOLS] - lower[:, TCOLS:], upper[:, TCOLS:] + lower[:, :TCOLS]], axis=1
        )

    offsets = [2, 1, 3][:bands - 1]
    for offset in offsets:
        other = lax.rem(band + offset, bands)
        send3[offset - 1] = tile_part(other).astype(BF16)
        pltpu.make_async_remote_copy(
            src_ref=send3.at[offset - 1], dst_ref=recv3.at[offset - 1],
            send_sem=send_sems.at[2], recv_sem=recv_sems.at[2],
            device_id={"freq": other}, device_id_type=MESH,
        ).start()
    total = tile_part(band)
    wait3 = settle(send3, recv3, 2, "freq", bands, bands - 1)
    wait3.wait_recv()
    for offset in offsets:
        total = total + recv3[offset - 1].astype(F32)
    t_real, t_imag = total[:, :TCOLS], total[:, TCOLS:]

    def turned(other):
        angle = jnp.zeros((1, TCOLS), I32) + ((my_class * other & (RADIX - 1)) << 13)
        cos_c, sin_c = turn(angle)
        return t_real * cos_c - t_imag * sin_c

    for offset in range(1, RADIX):
        other = lax.rem(my_class + offset, RADIX)
        send4[offset - 1] = turned(other).astype(BF16)
        pltpu.make_async_remote_copy(
            src_ref=send4.at[offset - 1], dst_ref=recv4.at[offset - 1],
            send_sem=send_sems.at[3], recv_sem=recv_sems.at[3],
            device_id={"facet": other * RADIX + my_column}, device_id_type=MESH,
        ).start()
    image = turned(my_class)
    wait4 = settle(send4, recv4, 3, "facet", facets, RADIX - 1)
    wait4.wait_recv()
    for offset in range(1, RADIX):
        image = image + recv4[offset - 1].astype(F32)
    out_ref[...] = image * scale

    for finished in (wait1, wait2, wait3, wait4):
        finished.wait_send()


def shards(visibility, row_target, row_cell, row_plane, kernel_table, subgrid_anchor):
    facets = lax.axis_size("facet")
    bands = lax.axis_size("freq")
    rows = visibility.shape[2]
    scale = 1.0 / (SUB * math.sqrt(facets * bands * rows))
    width = facets * KS
    band_rows = TROWS // bands
    vmem = pl.BlockSpec(memory_space=pltpu.VMEM)
    return pl.pallas_call(
        functools.partial(kernel, facets, bands, scale),
        out_shape=jax.ShapeDtypeStruct((band_rows, TCOLS), F32),
        in_specs=[vmem, vmem, vmem, vmem, pl.BlockSpec(memory_space=pltpu.SMEM), pl.BlockSpec(memory_space=pl.ANY)],
        out_specs=vmem,
        scratch_shapes=[
            pltpu.VMEM((2, PLANES * SUB, SUB), BF16),
            pltpu.VMEM((facets, 1, LANES), F32),
            pltpu.VMEM((facets, 1, LANES), F32),
            pltpu.VMEM((RADIX, 2 * SUB, 2 * TCOLS), BF16),
            pltpu.VMEM((facets, KS, 2 * TCOLS), BF16),
            pltpu.VMEM((facets, KS, 2 * TCOLS), BF16),
            pltpu.VMEM((bands, 2 * band_rows, width), BF16),
            pltpu.VMEM((bands - 1, band_rows, 2 * TCOLS), BF16),
            pltpu.VMEM((bands - 1, band_rows, 2 * TCOLS), BF16),
            pltpu.VMEM((RADIX - 1, band_rows, TCOLS), BF16),
            pltpu.VMEM((RADIX - 1, band_rows, TCOLS), BF16),
            pltpu.SemaphoreType.DMA,
            pltpu.SemaphoreType.DMA((4,)),
            pltpu.SemaphoreType.DMA((4,)),
        ],
        compiler_params=pltpu.CompilerParams(
            collective_id=0, has_side_effects=True, vmem_limit_bytes=60 * 1024 * 1024
        ),
        cost_estimate=pl.CostEstimate(flops=8 * 10**9, bytes_accessed=4 * 10**6, transcendentals=0),
    )(
        visibility[0], row_target.reshape(1, rows), row_cell, row_plane, subgrid_anchor, kernel_table
    )


def solution(mesh):
    placed = (
        P("freq", None, "facet"),
        P("freq", "facet", None),
        P("freq", "facet"),
        P("freq", "facet"),
        P(),
        P("facet", None),
    )
    return jax.shard_map(
        shards, mesh=mesh, in_specs=placed, out_specs=P(("facet", "freq"), None), check_vma=False
    )
```

```python
import functools
import math

import jax
import jax.numpy as jnp
from jax import lax
from jax.experimental import pallas as pl
from jax.experimental.pallas import tpu as pltpu
from jax.sharding import PartitionSpec as P

NGRID = 65536
TROWS = 1024
TCOLS = 128
SUB = 256
PLANES = 8
CAP = 16
RADIX = 8
LANES = 128
KS = SUB // RADIX
SECTIONS = 2
MESH = pl.DeviceIdType.MESH
F32, BF16, I32 = jnp.float32, jnp.bfloat16, jnp.int32


def turn(index):
    index = index & (NGRID - 1)
    quadrant = (index + NGRID // 8) >> 14
    rest = (index - (quadrant << 14)).astype(F32) * (2.0 * math.pi / NGRID)
    square = rest * rest
    sine = rest * (1.0 + square * (-1.0 / 6 + square * (1.0 / 120 + square * (-1.0 / 5040 + square * (1.0 / 362880)))))
    cosine = 1.0 + square * (-0.5 + square * (1.0 / 24 + square * (-1.0 / 720 + square * (1.0 / 40320))))
    odd = (quadrant & 1) == 1
    c = jnp.where(odd, sine, cosine)
    s = jnp.where(odd, cosine, sine)
    c = jnp.where(((quadrant + 1) & 2) == 2, -c, c)
    s = jnp.where((quadrant & 2) == 2, -s, s)
    return c, s


def iota(shape, dim):
    return lax.broadcasted_iota(I32, shape, dim)


def nt_dot(a, b):
    return lax.dot_general(a, b, (((1,), (1,)), ((), ())), preferred_element_type=F32)


def tn_dot(a, b):
    return lax.dot_general(a, b, (((0,), (0,)), ((), ())), preferred_element_type=F32)


def dot(a, b):
    return jnp.dot(a, b, preferred_element_type=F32)


def send(source, target, send_sem, recv_sem, device):
    copy = pltpu.make_async_remote_copy(
        src_ref=source, dst_ref=target, send_sem=send_sem, recv_sem=recv_sem,
        device_id=device, device_id_type=MESH,
    )
    copy.start()
    return copy


class RingSum:
    def __init__(self, chunk, up, down, out_ref, in_ref, send_sem, recv_sem):
        self.chunk, self.up, self.down = chunk, up, down
        self.out, self.came, self.send_sem, self.recv_sem = out_ref, in_ref, send_sem, recv_sem
        self.copies = []

    def go(self, slot, value, device):
        self.out[slot] = value.astype(BF16)
        copy = send(self.out.at[slot], self.came.at[slot], self.send_sem.at[slot], self.recv_sem.at[slot], device)
        self.copies.append(copy)

    def arrived(self, slot):
        self.copies[slot].wait_recv()
        return self.came[slot].astype(F32)

    def start(self):
        self.go(0, self.chunk(2, 0), self.up)
        self.go(1, self.chunk(2, 1), self.down)

    def plain(self):
        self.go(2, self.chunk(1, 1), self.up)
        self.go(3, self.chunk(3, 0), self.down)

    def middle(self):
        term_up, term_down = self.chunk(1, 0), self.chunk(3, 1)
        self.go(4, term_up + self.arrived(0), self.up)
        self.go(5, term_down + self.arrived(1), self.down)

    def finish(self):
        halves = [self.chunk(0, 0), self.chunk(0, 1)]
        halves = [halves[0] + self.arrived(3), halves[1] + self.arrived(2)]
        halves = [halves[0] + self.arrived(4), halves[1] + self.arrived(5)]
        return jnp.concatenate(halves, axis=0)


def kernel(
    facets, bands, scale,
    vis_ref, target_ref, cell_ref, plane_ref, anchor_ref, table_hbm, out_ref,
    table, ordered, send1, recv1, right, grid_out, grid_in, send2, recv2, left, part_out, part_in, last_out, last_in,
    table_sem, send_sems, recv_sems, grid_sems, part_sems, last_sems,
):
    me = lax.axis_index("facet")
    band = lax.axis_index("freq")
    my_class, my_column = me // RADIX, me % RADIX
    my_z, my_y = my_class // 4, my_class % 4
    rows = vis_ref.shape[1]
    cells = PLANES * SUB
    band_rows = TROWS // bands
    kept = KS // bands
    band_up = {"freq": lax.rem(band + 1, bands)}
    band_down = {"freq": lax.rem(band + bands - 1, bands)}

    load_table = pltpu.make_async_copy(table_hbm, table, table_sem)
    load_table.start()

    barrier = pltpu.get_barrier_semaphore()

    @pl.loop(1, facets)
    def _(offset):
        pl.semaphore_signal(
            barrier, inc=1, device_id={"facet": lax.rem(me + offset, facets)}, device_id_type=MESH
        )

    pl.semaphore_signal(barrier, inc=1, device_id=band_up, device_id_type=MESH)
    pl.semaphore_signal(barrier, inc=1, device_id=band_down, device_id_type=MESH)

    named = iota((facets, rows), 0) == target_ref[...]
    named_f = jnp.where(named, 1.0, 0.0)
    named_b = named_f.astype(BF16)
    earlier = jnp.where(iota((rows, rows), 0) < iota((rows, rows), 1), 1.0, 0.0).astype(BF16)
    position = jnp.sum(named_f * dot(named_b, earlier), axis=0, keepdims=True)
    here = iota((CAP, rows), 0).astype(F32) == position
    vis = vis_ref[...].astype(F32)
    cell = cell_ref[...]
    payloads = (
        vis[0:1], vis[1:2], (cell >> 8).astype(F32), (cell & 255).astype(F32), plane_ref[...].astype(F32),
    )
    spread = [jnp.where(here, payload, 0.0) for payload in payloads]
    spread.append(jnp.zeros((LANES - CAP * len(payloads), rows), F32))
    slots = nt_dot(named_b, jnp.concatenate(spread, axis=0).astype(BF16))
    lane = iota((facets, LANES), 1)
    us, vs = anchor_ref[0, 0], anchor_ref[0, 1]
    slots = jnp.where(lane == CAP * 5, us.astype(F32), slots)
    send1[...] = slots.reshape(facets, 1, LANES)
    recv1[pl.ds(me, 1)] = send1[pl.ds(me, 1)]

    pl.semaphore_wait(barrier, facets - 1 + 2)

    @pl.loop(1, facets)
    def _(offset):
        peer = lax.rem(me + offset, facets)
        send(send1.at[peer], recv1.at[me], send_sems.at[0], recv_sems.at[0], {"facet": peer})

    def settle(target, phase):
        return pltpu.make_async_remote_copy(
            src_ref=target.at[pl.ds(0, facets - 1)], dst_ref=target.at[pl.ds(0, facets - 1)],
            send_sem=send_sems.at[phase], recv_sem=recv_sems.at[phase],
            device_id={"facet": lax.rem(me + 1, facets)}, device_id_type=MESH,
        )

    for step in range(RADIX):
        group = lax.rem(my_column + step, RADIX)
        spatial = vs + iota((SUB, TCOLS), 0)
        pixel = iota((SUB, TCOLS), 1)
        index = (((spatial & (RADIX - 1)) * group & (RADIX - 1)) << 13) + spatial * pixel
        cos_r, sin_r = turn(index)
        cos_r, sin_r = cos_r.astype(BF16), sin_r.astype(BF16)
        at = step * 2 * TCOLS
        right[:SUB, at:at + TCOLS] = cos_r
        right[:SUB, at + TCOLS:at + 2 * TCOLS] = sin_r
        right[SUB:, at:at + TCOLS] = -sin_r
        right[SUB:, at + TCOLS:at + 2 * TCOLS] = cos_r

    load_table.wait()
    place = iota((SUB, SUB), 0)
    row_k = (((place >> 6) + band) & (bands - 1)) * kept + (place & (kept - 1))
    wanted = (row_k << 3) + ((((place >> 3) & (RADIX - 1)) - us) & (RADIX - 1))
    order = jnp.where(iota((SUB, SUB), 1) == wanted, 1.0, 0.0).astype(BF16)
    for part in range(2):
        ordered[part * SUB:(part + 1) * SUB] = nt_dot(order, table[part]).astype(BF16)

    wait1 = settle(recv1, 0)
    wait1.wait_recv()

    got = recv1[...].reshape(facets, LANES)
    v_cell = got[:, 3 * CAP:4 * CAP] + got[:, 4 * CAP:5 * CAP] * SUB
    every = iota((facets, cells), 1).astype(F32)
    pick_v = jnp.concatenate(
        [jnp.where(every == v_cell[:, q:q + 1], 1.0, 0.0).astype(BF16) for q in range(CAP)], axis=0
    )
    k_real = dot(pick_v, table[0])
    k_imag = dot(pick_v, table[1])
    v_real = jnp.concatenate([got[:, q:q + 1] for q in range(CAP)], axis=0)
    v_imag = jnp.concatenate([got[:, CAP + q:CAP + q + 1] for q in range(CAP)], axis=0)
    b_real = (v_real * k_real - v_imag * k_imag).astype(BF16)
    b_imag = (v_real * k_imag + v_imag * k_real).astype(BF16)
    flat = got.T
    u_row = jnp.concatenate([flat[2 * CAP + q:2 * CAP + q + 1] for q in range(CAP)], axis=1)
    plane_row = jnp.concatenate([flat[4 * CAP + q:4 * CAP + q + 1] for q in range(CAP)], axis=1)
    pick_u = jnp.where(iota((SUB, facets * CAP), 0).astype(F32) == u_row, 1.0, 0.0).astype(BF16)
    pick_u = jnp.concatenate(
        [pick_u * jnp.where(plane_row == p, 1.0, 0.0).astype(BF16) for p in range(PLANES)], axis=0
    )
    a_both = dot(ordered[...], pick_u).astype(BF16)
    b_wide = jnp.concatenate([b_real, b_imag], axis=1)
    b_turned = jnp.concatenate([-b_imag, b_real], axis=1)
    quarter = SUB // bands
    gridded = dot(a_both[:SUB], b_wide) + dot(a_both[SUB:], b_turned)

    def grid_chunk(r, h):
        start = r * quarter + h * (quarter // 2)
        return gridded[start:start + quarter // 2]

    width = facets * 2 * kept
    own_s = iota((facets, width), 0) == (iota((facets, width), 1) >> 4)
    first = jnp.sum(jnp.where(own_s, got[:, 5 * CAP:5 * CAP + 1], 0.0), axis=0, keepdims=True).astype(I32)
    first = first + ((my_class - first) & (RADIX - 1))
    column = iota((1, width), 1)
    spatial = first + (((column & (kept - 1)) + band * kept) << 3)
    ahead = ((column >> 3) & 1) << 14
    fine = 32
    pieces = band_rows // fine
    coarse = iota((bands * pieces, width), 0)
    coarse = ((((coarse >> 3) + band) & (bands - 1)) << 3) + (coarse & (pieces - 1))

    def make_left(blocks):
        for piece in range(blocks[0] * pieces, (blocks[-1] + 1) * pieces):
            p_r, p_i = coarse_r[piece:piece + 1], coarse_i[piece:piece + 1]
            block, at = piece // pieces, piece % pieces * fine
            left[block, 0, at:at + fine] = (p_r * fine_r - p_i * fine_i).astype(BF16)
            left[block, 1, at:at + fine] = (p_r * fine_i + p_i * fine_r).astype(BF16)

    ring = RingSum(grid_chunk, band_up, band_down, grid_out, grid_in, grid_sems.at[0], grid_sems.at[1])
    ring.start()
    ring.plain()
    coarse_r, coarse_i = turn(coarse * fine * spatial)
    fine_r, fine_i = turn(iota((fine, width), 0) * spatial + ahead)
    ring.middle()
    make_left(range(bands))
    grid = ring.finish().astype(BF16)

    share = RADIX // 2
    for part in range(2):
        span = share * 2 * TCOLS
        half = dot(grid, right[:, part * span:(part + 1) * span])
        for step in range(share):
            at = step * 2 * TCOLS
            pieces = [half[:, at + p * TCOLS:at + (p + 1) * TCOLS].reshape(RADIX, kept, TCOLS) for p in range(2)]
            send2[part * share + step] = jnp.concatenate(pieces, axis=1).astype(BF16)

        @pl.loop(0, share * RADIX)
        def _(number):
            step, turn_by = part * share + number // RADIX, number % RADIX
            peer_class = lax.rem(my_class + turn_by, RADIX)
            peer = peer_class * RADIX + lax.rem(my_column + step, RADIX)

            @pl.when(peer != me)
            def _():
                send(send2.at[step, peer_class], recv2.at[me], send_sems.at[1], recv_sems.at[1], {"facet": peer})

    recv2[pl.ds(me, 1)] = send2[0, pl.ds(my_class, 1)]

    wait2 = settle(recv2, 1)
    wait2.wait_recv()

    mixed = recv2[...].reshape(width, TCOLS)
    sections = part_out.shape[0]
    section_rows = band_rows // sections
    half_rows = section_rows // 2
    y_up, y_down = lax.rem(my_y + 1, 4), lax.rem(my_y + 3, 4)
    across = lax.rem(my_y + 2, 4)

    def tile_part(section, r, h):
        at = section * section_rows + h * half_rows
        return jnp.concatenate([dot(left[r, p, at:at + half_rows], mixed) for p in range(2)], axis=1)

    def phase(z, y):
        return turn(jnp.zeros((1, TCOLS), I32) + ((my_class * (4 * z + y) & (RADIX - 1)) << 13))

    phases = {(z, n): phase(z, y) for z in range(2) for n, y in enumerate((my_y, y_up, across, y_down))}
    phases["pair"], phases["own"] = phase(1 - my_z, my_y), phase(my_z, my_y)

    class Last:
        def __init__(self, section, total):
            self.real, self.imag = total[:, :TCOLS], total[:, TCOLS:]
            self.out, self.came = last_out.at[section], last_in.at[section]
            self.send_sem, self.recv_sem = last_sems.at[0, section], last_sems.at[1, section]
            self.copies = []

        def turned(self, key):
            return self.real * phases[key][0] - self.imag * phases[key][1]

        def go(self, out_slot, in_slot, value, z, y):
            self.out[out_slot] = value.astype(BF16)
            copy = send(
                self.out.at[out_slot], self.came.at[in_slot], self.send_sem.at[out_slot], self.recv_sem.at[in_slot],
                {"facet": (z * 4 + y) * RADIX + my_column},
            )
            self.copies.append(copy)

        def arrived(self, slot):
            pltpu.make_async_remote_copy(
                src_ref=self.out.at[slot], dst_ref=self.came.at[slot], send_sem=self.send_sem.at[slot],
                recv_sem=self.recv_sem.at[slot], device_id={"facet": lax.rem(me + 1, facets)}, device_id_type=MESH,
            ).wait_recv()
            return self.came[slot].astype(F32)

        def start(self):
            self.go(0, 0, self.turned((0, 2)), my_z, y_up)
            self.go(1, 1, self.turned((1, 2)), my_z, y_down)
            self.go(2, 2 + my_z, self.turned((1, 1)), 1, y_up)
            self.go(3, 4 + my_z, self.turned((0, 3)), 0, y_down)
            self.go(6, 6, self.turned("pair"), 1 - my_z, my_y)

        def middle(self):
            term_up, term_down = self.turned((0, 1)), self.turned((1, 3))
            self.go(4, 2 + my_z, term_up + self.arrived(0), 0, y_up)
            self.go(5, 4 + my_z, term_down + self.arrived(1), 1, y_down)

        def finish(self):
            image = self.turned("own")
            for slot in range(2, 7):
                image = image + self.arrived(slot)
            return image

    rings = [
        RingSum(
            functools.partial(tile_part, section), band_up, band_down,
            part_out.at[section], part_in.at[section], part_sems.at[0, section], part_sems.at[1, section],
        )
        for section in range(sections)
    ]
    for each in rings:
        each.start()
    for each in rings:
        each.plain()
    for each in rings:
        each.middle()
    lasts = []
    for section, each in enumerate(rings):
        lasts.append(Last(section, each.finish()))
        lasts[-1].start()
        if section:
            lasts[section - 1].middle()
    lasts[-1].middle()
    for section, each in enumerate(lasts):
        out_ref[section * section_rows:(section + 1) * section_rows] = each.finish() * scale

    for finished in [wait1, wait2]:
        finished.wait_send()
    for each in [ring, *rings, *lasts]:
        for copy in each.copies:
            copy.wait_send()


def shards(visibility, row_target, row_cell, row_plane, kernel_table, subgrid_anchor):
    facets = lax.axis_size("facet")
    bands = lax.axis_size("freq")
    rows = visibility.shape[2]
    scale = 1.0 / (SUB * math.sqrt(facets * bands * rows))
    kept = KS // bands
    band_rows = TROWS // bands
    vmem = pl.BlockSpec(memory_space=pltpu.VMEM)
    return pl.pallas_call(
        functools.partial(kernel, facets, bands, scale),
        out_shape=jax.ShapeDtypeStruct((band_rows, TCOLS), F32),
        in_specs=[vmem, vmem, vmem, vmem, pl.BlockSpec(memory_space=pltpu.SMEM), pl.BlockSpec(memory_space=pl.ANY)],
        out_specs=vmem,
        scratch_shapes=[
            pltpu.VMEM((2, PLANES * SUB, SUB), BF16),
            pltpu.VMEM((2 * SUB, PLANES * SUB), BF16),
            pltpu.VMEM((facets, 1, LANES), F32),
            pltpu.VMEM((facets, 1, LANES), F32),
            pltpu.VMEM((2 * SUB, RADIX * 2 * TCOLS), BF16),
            pltpu.VMEM((6, SUB // bands // 2, 2 * SUB), BF16),
            pltpu.VMEM((6, SUB // bands // 2, 2 * SUB), BF16),
            pltpu.VMEM((RADIX, RADIX, 2 * kept, TCOLS), BF16),
            pltpu.VMEM((facets, 2 * kept, TCOLS), BF16),
            pltpu.VMEM((bands, 2, band_rows, facets * 2 * kept), BF16),
            pltpu.VMEM((SECTIONS, 6, band_rows // SECTIONS // 2, 2 * TCOLS), BF16),
            pltpu.VMEM((SECTIONS, 6, band_rows // SECTIONS // 2, 2 * TCOLS), BF16),
            pltpu.VMEM((SECTIONS, 7, band_rows // SECTIONS, TCOLS), BF16),
            pltpu.VMEM((SECTIONS, 7, band_rows // SECTIONS, TCOLS), BF16),
            pltpu.SemaphoreType.DMA,
            pltpu.SemaphoreType.DMA((2,)),
            pltpu.SemaphoreType.DMA((2,)),
            pltpu.SemaphoreType.DMA((2, 6)),
            pltpu.SemaphoreType.DMA((2, SECTIONS, 6)),
            pltpu.SemaphoreType.DMA((2, SECTIONS, 7)),
        ],
        compiler_params=pltpu.CompilerParams(
            collective_id=0, has_side_effects=True, vmem_limit_bytes=60 * 1024 * 1024
        ),
        cost_estimate=pl.CostEstimate(flops=8 * 10**9, bytes_accessed=4 * 10**6, transcendentals=0),
    )(
        visibility[0], row_target.reshape(1, rows), row_cell, row_plane, subgrid_anchor, kernel_table
    )


def solution(mesh):
    placed = (
        P("freq", None, "facet"),
        P("freq", "facet", None),
        P("freq", "facet"),
        P("freq", "facet"),
        P(),
        P("facet", None),
    )
    return jax.shard_map(
        shards, mesh=mesh, in_specs=placed, out_specs=P(("facet", "freq"), None), check_vma=False
    )
```

```python
import functools
import math

import jax
import jax.numpy as jnp
from jax import lax
from jax.experimental import pallas as pl
from jax.experimental.pallas import tpu as pltpu
from jax.sharding import PartitionSpec as P

NGRID = 65536
TROWS = 1024
TCOLS = 128
SUB = 256
PLANES = 8
CAP = 16
RADIX = 8
LANES = 128
KS = SUB // RADIX
SECTIONS = 2
MESH = pl.DeviceIdType.MESH
F32, BF16, I32 = jnp.float32, jnp.bfloat16, jnp.int32


def turn(index):
    index = index & (NGRID - 1)
    quadrant = (index + NGRID // 8) >> 14
    rest = (index - (quadrant << 14)).astype(F32) * (2.0 * math.pi / NGRID)
    square = rest * rest
    sine = rest * (1.0 + square * (-1.0 / 6 + square * (1.0 / 120 + square * (-1.0 / 5040 + square * (1.0 / 362880)))))
    cosine = 1.0 + square * (-0.5 + square * (1.0 / 24 + square * (-1.0 / 720 + square * (1.0 / 40320))))
    odd = (quadrant & 1) == 1
    c = jnp.where(odd, sine, cosine)
    s = jnp.where(odd, cosine, sine)
    c = jnp.where(((quadrant + 1) & 2) == 2, -c, c)
    s = jnp.where((quadrant & 2) == 2, -s, s)
    return c, s


def iota(shape, dim):
    return lax.broadcasted_iota(I32, shape, dim)


def nt_dot(a, b):
    return lax.dot_general(a, b, (((1,), (1,)), ((), ())), preferred_element_type=F32)


def tn_dot(a, b):
    return lax.dot_general(a, b, (((0,), (0,)), ((), ())), preferred_element_type=F32)


def dot(a, b):
    return jnp.dot(a, b, preferred_element_type=F32)


def send(source, target, send_sem, recv_sem, device):
    copy = pltpu.make_async_remote_copy(
        src_ref=source, dst_ref=target, send_sem=send_sem, recv_sem=recv_sem,
        device_id=device, device_id_type=MESH,
    )
    copy.start()
    return copy


class RingSum:
    def __init__(self, chunk, up, down, out_ref, in_ref, send_sem, recv_sem):
        self.chunk, self.up, self.down = chunk, up, down
        self.out, self.came, self.send_sem, self.recv_sem = out_ref, in_ref, send_sem, recv_sem
        self.copies = []

    def go(self, slot, value, device):
        self.out[slot] = value.astype(BF16)
        copy = send(self.out.at[slot], self.came.at[slot], self.send_sem.at[slot], self.recv_sem.at[slot], device)
        self.copies.append(copy)

    def arrived(self, slot):
        self.copies[slot].wait_recv()
        return self.came[slot].astype(F32)

    def start(self):
        self.go(0, self.chunk(2, 0), self.up)
        self.go(1, self.chunk(2, 1), self.down)

    def plain(self):
        self.go(2, self.chunk(1, 1), self.up)
        self.go(3, self.chunk(3, 0), self.down)

    def middle(self):
        term_up, term_down = self.chunk(1, 0), self.chunk(3, 1)
        self.go(4, term_up + self.arrived(0), self.up)
        self.go(5, term_down + self.arrived(1), self.down)

    def finish(self):
        halves = [self.chunk(0, 0), self.chunk(0, 1)]
        halves = [halves[0] + self.arrived(3), halves[1] + self.arrived(2)]
        halves = [halves[0] + self.arrived(4), halves[1] + self.arrived(5)]
        return jnp.concatenate(halves, axis=0)


def kernel(
    facets, bands, scale,
    vis_ref, target_ref, cell_ref, plane_ref, anchor_ref, table_hbm, out_ref,
    table, ordered, send1, recv1, right, grid_out, grid_in, send2, recv2, left, part_out, part_in, last_out, last_in,
    table_sem, send_sems, recv_sems, grid_sems, part_sems, last_sems,
):
    me = lax.axis_index("facet")
    band = lax.axis_index("freq")
    my_share, my_column = me // RADIX, me % RADIX
    my_z, my_y = my_share // 4, my_share % 4
    special = jnp.where(my_y == 0, 1, 0)
    rows = vis_ref.shape[1]
    cells = PLANES * SUB
    band_rows = TROWS // bands
    kept = KS // bands
    band_up = {"freq": lax.rem(band + 1, bands)}
    band_down = {"freq": lax.rem(band + bands - 1, bands)}

    load_table = pltpu.make_async_copy(table_hbm, table, table_sem)
    load_table.start()

    barrier = pltpu.get_barrier_semaphore()

    @pl.loop(1, facets)
    def _(offset):
        pl.semaphore_signal(
            barrier, inc=1, device_id={"facet": lax.rem(me + offset, facets)}, device_id_type=MESH
        )

    pl.semaphore_signal(barrier, inc=1, device_id=band_up, device_id_type=MESH)
    pl.semaphore_signal(barrier, inc=1, device_id=band_down, device_id_type=MESH)

    named = iota((facets, rows), 0) == target_ref[...]
    named_f = jnp.where(named, 1.0, 0.0)
    named_b = named_f.astype(BF16)
    earlier = jnp.where(iota((rows, rows), 0) < iota((rows, rows), 1), 1.0, 0.0).astype(BF16)
    position = jnp.sum(named_f * dot(named_b, earlier), axis=0, keepdims=True)
    here = iota((CAP, rows), 0).astype(F32) == position
    vis = vis_ref[...].astype(F32)
    cell = cell_ref[...]
    payloads = (
        vis[0:1], vis[1:2], (cell >> 8).astype(F32), (cell & 255).astype(F32), plane_ref[...].astype(F32),
    )
    spread = [jnp.where(here, payload, 0.0) for payload in payloads]
    spread.append(jnp.zeros((LANES - CAP * len(payloads), rows), F32))
    slots = nt_dot(named_b, jnp.concatenate(spread, axis=0).astype(BF16))
    lane = iota((facets, LANES), 1)
    us, vs = anchor_ref[0, 0], anchor_ref[0, 1]
    slots = jnp.where(lane == CAP * 5, us.astype(F32), slots)
    send1[...] = slots.reshape(facets, 1, LANES)
    recv1[pl.ds(me, 1)] = send1[pl.ds(me, 1)]

    pl.semaphore_wait(barrier, facets - 1 + 2)

    @pl.loop(1, facets)
    def _(offset):
        peer = lax.rem(me + offset, facets)
        send(send1.at[peer], recv1.at[me], send_sems.at[0], recv_sems.at[0], {"facet": peer})

    def settle(target, phase):
        return pltpu.make_async_remote_copy(
            src_ref=target.at[pl.ds(0, facets - 1)], dst_ref=target.at[pl.ds(0, facets - 1)],
            send_sem=send_sems.at[phase], recv_sem=recv_sems.at[phase],
            device_id={"facet": lax.rem(me + 1, facets)}, device_id_type=MESH,
        )

    low = iota((1, TCOLS), 1) < TCOLS // 2

    def swap(value):
        return pltpu.roll(value, TCOLS // 2, 1)

    for step in range(RADIX):
        group = lax.rem(my_column + step, RADIX)
        spatial = vs + iota((SUB, TCOLS), 0)
        pixel = iota((SUB, TCOLS), 1)
        index = (((spatial & (RADIX - 1)) * group & (RADIX - 1)) << 13) + spatial * pixel
        cos_r, sin_r = turn(index)
        cos_s, sin_s = swap(cos_r), swap(sin_r)
        at = step * 2 * TCOLS
        right[:SUB, at:at + TCOLS] = jnp.where(low, cos_r, sin_s).astype(BF16)
        right[:SUB, at + TCOLS:at + 2 * TCOLS] = jnp.where(low, cos_s, sin_r).astype(BF16)
        right[SUB:, at:at + TCOLS] = jnp.where(low, -sin_r, cos_s).astype(BF16)
        right[SUB:, at + TCOLS:at + 2 * TCOLS] = jnp.where(low, -sin_s, cos_r).astype(BF16)

    load_table.wait()
    place = iota((SUB, SUB), 0)
    row_k = (((place >> 6) + band) & (bands - 1)) * kept + (place & (kept - 1))
    wanted = (row_k << 3) + ((((place >> 3) & (RADIX - 1)) - us) & (RADIX - 1))
    order = jnp.where(iota((SUB, SUB), 1) == wanted, 1.0, 0.0).astype(BF16)
    for part in range(2):
        ordered[part * SUB:(part + 1) * SUB] = nt_dot(order, table[part]).astype(BF16)

    wait1 = settle(recv1, 0)
    wait1.wait_recv()

    got = recv1[...].reshape(facets, LANES)
    v_cell = got[:, 3 * CAP:4 * CAP] + got[:, 4 * CAP:5 * CAP] * SUB
    every = iota((facets, cells), 1).astype(F32)
    pick_v = jnp.concatenate(
        [jnp.where(every == v_cell[:, q:q + 1], 1.0, 0.0).astype(BF16) for q in range(CAP)], axis=0
    )
    k_real = dot(pick_v, table[0])
    k_imag = dot(pick_v, table[1])
    v_real = jnp.concatenate([got[:, q:q + 1] for q in range(CAP)], axis=0)
    v_imag = jnp.concatenate([got[:, CAP + q:CAP + q + 1] for q in range(CAP)], axis=0)
    b_real = (v_real * k_real - v_imag * k_imag).astype(BF16)
    b_imag = (v_real * k_imag + v_imag * k_real).astype(BF16)
    flat = got.T
    u_row = jnp.concatenate([flat[2 * CAP + q:2 * CAP + q + 1] for q in range(CAP)], axis=1)
    plane_row = jnp.concatenate([flat[4 * CAP + q:4 * CAP + q + 1] for q in range(CAP)], axis=1)
    pick_u = jnp.where(iota((SUB, facets * CAP), 0).astype(F32) == u_row, 1.0, 0.0).astype(BF16)
    pick_u = jnp.concatenate(
        [pick_u * jnp.where(plane_row == p, 1.0, 0.0).astype(BF16) for p in range(PLANES)], axis=0
    )
    a_both = dot(ordered[...], pick_u).astype(BF16)
    b_wide = jnp.concatenate([b_real, b_imag], axis=1)
    b_turned = jnp.concatenate([-b_imag, b_real], axis=1)
    quarter = SUB // bands
    gridded = dot(a_both[:SUB], b_wide) + dot(a_both[SUB:], b_turned)

    def grid_chunk(r, h):
        start = r * quarter + h * (quarter // 2)
        return gridded[start:start + quarter // 2]

    width = facets * 2 * kept
    own_s = iota((facets, width), 0) == (iota((facets, width), 1) >> 4)
    first = jnp.sum(jnp.where(own_s, got[:, 5 * CAP:5 * CAP + 1], 0.0), axis=0, keepdims=True).astype(I32)
    column = iota((1, width), 1)
    second = (column >> 3) & 1
    wanted = my_y + second * (RADIX - 2 * my_y)
    sign = 1 - 2 * second * (1 - special)
    fine = 32
    pieces = band_rows // fine
    coarse = iota((bands * pieces, width), 0)
    coarse = ((((coarse >> 3) + band) & (bands - 1)) << 3) + (coarse & (pieces - 1))

    def tables(residue, ahead):
        spatial = first + ((residue - first) & (RADIX - 1)) + (((column & (kept - 1)) + band * kept) << 3)
        spatial = (spatial * sign) & (NGRID - 1)
        return *turn(coarse * fine * spatial), *turn(iota((fine, width), 0) * spatial + ahead)

    def make_left():
        for piece in range(bands * pieces):
            block, at = piece // pieces, piece % pieces * fine
            c_r, c_i, f_r, f_i = tables_cos
            left[block, 0, at:at + fine] = (c_r[piece:piece + 1] * f_r - c_i[piece:piece + 1] * f_i).astype(BF16)
            c_r, c_i, f_r, f_i = tables_sin
            left[block, 1, at:at + fine] = (c_r[piece:piece + 1] * f_i + c_i[piece:piece + 1] * f_r).astype(BF16)

    ring = RingSum(grid_chunk, band_up, band_down, grid_out, grid_in, grid_sems.at[0], grid_sems.at[1])
    ring.start()
    ring.plain()
    tables_cos = tables(wanted, (special * second) << 14)
    tables_sin = tables(wanted + 4 * special, (special * (second + 1)) << 14)
    ring.middle()
    make_left()
    grid = ring.finish().astype(BF16)

    some = RADIX // 2
    conjugate = jnp.where(low, 1.0, -1.0)
    for part in range(2):
        span = some * 2 * TCOLS
        half = dot(grid, right[:, part * span:(part + 1) * span])
        for step in range(some):
            for z in range(2):
                at = (step * 2 + z) * TCOLS
                rows_of = [half[c * kept:(c + 1) * kept, at:at + TCOLS] for c in range(RADIX)]
                shares = [
                    (jnp.where(low, rows_of[0], swap(rows_of[4])), jnp.where(low, swap(rows_of[0]), rows_of[4])),
                    *((rows_of[c], rows_of[RADIX - c] * conjugate) for c in range(1, 4)),
                ]
                for y in range(4):
                    send2[part * some + step, z * 4 + y] = jnp.concatenate(shares[y], axis=0).astype(BF16)

        @pl.loop(0, some * RADIX)
        def _(number):
            step, turn_by = part * some + number // RADIX, number % RADIX
            peer_share = lax.rem(my_share + turn_by, RADIX)
            peer = peer_share * RADIX + lax.rem(my_column + step, RADIX)

            @pl.when(peer != me)
            def _():
                send(send2.at[step, peer_share], recv2.at[me], send_sems.at[1], recv_sems.at[1], {"facet": peer})

    recv2[pl.ds(me, 1)] = send2[0, pl.ds(my_share, 1)]

    wait2 = settle(recv2, 1)
    wait2.wait_recv()

    mixed = recv2[...].reshape(width, TCOLS)
    sections = part_out.shape[0]
    section_rows = band_rows // sections
    half_rows = section_rows // 2
    y_up, y_down = lax.rem(my_y + 1, 4), lax.rem(my_y + 3, 4)
    across = lax.rem(my_y + 2, 4)

    spec = special.astype(F32)
    below = jnp.where(low, 1.0, 0.0)
    plain = 1.0 - spec * (1.0 - below)
    kept_sine = spec * (1.0 - below)
    turned_sine = (1.0 - spec) * (1.0 - 2.0 * below)

    def tile_part(section, r, h):
        at = section * section_rows + h * half_rows
        cosines, sines = [dot(left[r, p, at:at + half_rows], mixed) for p in range(2)]
        return cosines * plain + sines * kept_sine + swap(sines) * turned_sine

    def phase(z, y):
        cos_c, sin_c = turn(jnp.zeros((1, TCOLS), I32) + ((my_y * (4 * z + y) & (RADIX - 1)) << 13))
        other = special * (1 - 2 * (y & 1))
        other = other.astype(F32) - sin_c
        return jnp.where(low, cos_c, other), jnp.where(low, other, cos_c)

    phases = {(z, n): phase(z, y) for z in range(2) for n, y in enumerate((my_y, y_up, across, y_down))}
    phases["pair"], phases["own"] = phase(1 - my_z, my_y), phase(my_z, my_y)

    class Last:
        def __init__(self, section, total):
            self.total, self.swapped = total, swap(total)
            self.out, self.came = last_out.at[section], last_in.at[section]
            self.send_sem, self.recv_sem = last_sems.at[0, section], last_sems.at[1, section]
            self.copies = []

        def turned(self, key):
            both = self.total * phases[key][0] + self.swapped * phases[key][1]
            return jnp.where(low, both[:half_rows], both[half_rows:])

        def go(self, out_slot, in_slot, value, z, y):
            self.out[out_slot] = value.astype(BF16)
            copy = send(
                self.out.at[out_slot], self.came.at[in_slot], self.send_sem.at[out_slot], self.recv_sem.at[in_slot],
                {"facet": (z * 4 + y) * RADIX + my_column},
            )
            self.copies.append(copy)

        def arrived(self, slot):
            pltpu.make_async_remote_copy(
                src_ref=self.out.at[slot], dst_ref=self.came.at[slot], send_sem=self.send_sem.at[slot],
                recv_sem=self.recv_sem.at[slot], device_id={"facet": lax.rem(me + 1, facets)}, device_id_type=MESH,
            ).wait_recv()
            return self.came[slot].astype(F32)

        def start(self):
            self.go(0, 0, self.turned((0, 2)), my_z, y_up)
            self.go(1, 1, self.turned((1, 2)), my_z, y_down)
            self.go(2, 2 + my_z, self.turned((1, 1)), 1, y_up)
            self.go(3, 4 + my_z, self.turned((0, 3)), 0, y_down)
            self.go(6, 6, self.turned("pair"), 1 - my_z, my_y)

        def middle(self):
            term_up, term_down = self.turned((0, 1)), self.turned((1, 3))
            self.go(4, 2 + my_z, term_up + self.arrived(0), 0, y_up)
            self.go(5, 4 + my_z, term_down + self.arrived(1), 1, y_down)

        def finish(self):
            came = [None, None, *(self.arrived(slot) for slot in range(2, 7))]
            own = self.turned("own")
            first = came[2] + came[4] + jnp.where(my_z == 0, own, came[6])
            other = came[3] + came[5] + jnp.where(my_z == 0, came[6], own)
            return jnp.concatenate(
                [jnp.where(low, first, swap(other)), jnp.where(low, swap(first), other)], axis=0
            )

    rings = [
        RingSum(
            functools.partial(tile_part, section), band_up, band_down,
            part_out.at[section], part_in.at[section], part_sems.at[0, section], part_sems.at[1, section],
        )
        for section in range(sections)
    ]
    for each in rings:
        each.start()
    for each in rings:
        each.plain()
    for each in rings:
        each.middle()
    lasts = []
    for section, each in enumerate(rings):
        lasts.append(Last(section, each.finish()))
        lasts[-1].start()
        if section:
            lasts[section - 1].middle()
    lasts[-1].middle()
    for section, each in enumerate(lasts):
        out_ref[section * section_rows:(section + 1) * section_rows] = each.finish() * scale

    for finished in [wait1, wait2]:
        finished.wait_send()
    for each in [ring, *rings, *lasts]:
        for copy in each.copies:
            copy.wait_send()


def shards(visibility, row_target, row_cell, row_plane, kernel_table, subgrid_anchor):
    facets = lax.axis_size("facet")
    bands = lax.axis_size("freq")
    rows = visibility.shape[2]
    scale = 1.0 / (SUB * math.sqrt(facets * bands * rows))
    kept = KS // bands
    band_rows = TROWS // bands
    vmem = pl.BlockSpec(memory_space=pltpu.VMEM)
    return pl.pallas_call(
        functools.partial(kernel, facets, bands, scale),
        out_shape=jax.ShapeDtypeStruct((band_rows, TCOLS), F32),
        in_specs=[vmem, vmem, vmem, vmem, pl.BlockSpec(memory_space=pltpu.SMEM), pl.BlockSpec(memory_space=pl.ANY)],
        out_specs=vmem,
        scratch_shapes=[
            pltpu.VMEM((2, PLANES * SUB, SUB), BF16),
            pltpu.VMEM((2 * SUB, PLANES * SUB), BF16),
            pltpu.VMEM((facets, 1, LANES), F32),
            pltpu.VMEM((facets, 1, LANES), F32),
            pltpu.VMEM((2 * SUB, RADIX * 2 * TCOLS), BF16),
            pltpu.VMEM((6, SUB // bands // 2, 2 * SUB), BF16),
            pltpu.VMEM((6, SUB // bands // 2, 2 * SUB), BF16),
            pltpu.VMEM((RADIX, RADIX, 2 * kept, TCOLS), BF16),
            pltpu.VMEM((facets, 2 * kept, TCOLS), BF16),
            pltpu.VMEM((bands, 2, band_rows, facets * 2 * kept), BF16),
            pltpu.VMEM((SECTIONS, 6, band_rows // SECTIONS // 2, TCOLS), BF16),
            pltpu.VMEM((SECTIONS, 6, band_rows // SECTIONS // 2, TCOLS), BF16),
            pltpu.VMEM((SECTIONS, 7, band_rows // SECTIONS // 2, TCOLS), BF16),
            pltpu.VMEM((SECTIONS, 7, band_rows // SECTIONS // 2, TCOLS), BF16),
            pltpu.SemaphoreType.DMA,
            pltpu.SemaphoreType.DMA((2,)),
            pltpu.SemaphoreType.DMA((2,)),
            pltpu.SemaphoreType.DMA((2, 6)),
            pltpu.SemaphoreType.DMA((2, SECTIONS, 6)),
            pltpu.SemaphoreType.DMA((2, SECTIONS, 7)),
        ],
        compiler_params=pltpu.CompilerParams(
            collective_id=0, has_side_effects=True, vmem_limit_bytes=60 * 1024 * 1024
        ),
        cost_estimate=pl.CostEstimate(flops=8 * 10**9, bytes_accessed=4 * 10**6, transcendentals=0),
    )(
        visibility[0], row_target.reshape(1, rows), row_cell, row_plane, subgrid_anchor, kernel_table
    )


def solution(mesh):
    placed = (
        P("freq", None, "facet"),
        P("freq", "facet", None),
        P("freq", "facet"),
        P("freq", "facet"),
        P(),
        P("facet", None),
    )
    return jax.shard_map(
        shards, mesh=mesh, in_specs=placed, out_specs=P(("facet", "freq"), None), check_vma=False
    )
```

```python
import functools
import math

import jax
import jax.numpy as jnp
from jax import lax
from jax.experimental import pallas as pl
from jax.experimental.pallas import tpu as pltpu
from jax.sharding import PartitionSpec as P

NGRID = 65536
TROWS = 1024
TCOLS = 128
SUB = 256
PLANES = 8
CAP = 16
RADIX = 8
LANES = 128
KS = SUB // RADIX
SECTIONS = 2
PLACES = sorted(
    ((z, y, x, c) for z in range(2) for y in range(4) for x in range(4) for c in range(2) if z + y + x + c),
    key=lambda p: -(2 * p[0] + 2 * min(p[1], 4 - p[1]) + 2 * min(p[2], 4 - p[2]) + p[3]),
)
COLUMNS = tuple((x, c) for x in (2, 1, 3, 0) for c in (1, 0))
MESH = pl.DeviceIdType.MESH
F32, BF16, I32 = jnp.float32, jnp.bfloat16, jnp.int32


def turn(index):
    index = index & (NGRID - 1)
    quadrant = (index + NGRID // 8) >> 14
    rest = (index - (quadrant << 14)).astype(F32) * (2.0 * math.pi / NGRID)
    square = rest * rest
    sine = rest * (1.0 + square * (-1.0 / 6 + square * (1.0 / 120 + square * (-1.0 / 5040 + square * (1.0 / 362880)))))
    cosine = 1.0 + square * (-0.5 + square * (1.0 / 24 + square * (-1.0 / 720 + square * (1.0 / 40320))))
    odd = (quadrant & 1) == 1
    c = jnp.where(odd, sine, cosine)
    s = jnp.where(odd, cosine, sine)
    c = jnp.where(((quadrant + 1) & 2) == 2, -c, c)
    s = jnp.where((quadrant & 2) == 2, -s, s)
    return c, s


def iota(shape, dim):
    return lax.broadcasted_iota(I32, shape, dim)


def nt_dot(a, b):
    return lax.dot_general(a, b, (((1,), (1,)), ((), ())), preferred_element_type=F32)


def tn_dot(a, b):
    return lax.dot_general(a, b, (((0,), (0,)), ((), ())), preferred_element_type=F32)


def dot(a, b):
    return jnp.dot(a, b, preferred_element_type=F32)


def send(source, target, send_sem, recv_sem, device):
    copy = pltpu.make_async_remote_copy(
        src_ref=source, dst_ref=target, send_sem=send_sem, recv_sem=recv_sem,
        device_id=device, device_id_type=MESH,
    )
    copy.start()
    return copy


class RingSum:
    def __init__(self, chunk, up, down, out_ref, in_ref, send_sem, recv_sem):
        self.chunk, self.up, self.down = chunk, up, down
        self.out, self.came, self.send_sem, self.recv_sem = out_ref, in_ref, send_sem, recv_sem
        self.copies = []

    def go(self, slot, value, device):
        self.out[slot] = value.astype(BF16)
        copy = send(self.out.at[slot], self.came.at[slot], self.send_sem.at[slot], self.recv_sem.at[slot], device)
        self.copies.append(copy)

    def arrived(self, slot):
        self.copies[slot].wait_recv()
        return self.came[slot].astype(F32)

    def start(self):
        self.go(0, self.chunk(2, 0), self.up)
        self.go(1, self.chunk(2, 1), self.down)

    def plain(self):
        self.go(2, self.chunk(1, 1), self.up)
        self.go(3, self.chunk(3, 0), self.down)

    def middle(self):
        term_up, term_down = self.chunk(1, 0), self.chunk(3, 1)
        self.go(4, term_up + self.arrived(0), self.up)
        self.go(5, term_down + self.arrived(1), self.down)

    def finish(self):
        halves = [self.chunk(0, 0), self.chunk(0, 1)]
        halves = [halves[0] + self.arrived(3), halves[1] + self.arrived(2)]
        halves = [halves[0] + self.arrived(4), halves[1] + self.arrived(5)]
        return jnp.concatenate(halves, axis=0)


def kernel(
    facets, bands, scale,
    vis_hbm, target_hbm, cell_hbm, plane_hbm, anchor_hbm, table_hbm, out_ref,
    vis_ref, target_ref, cell_ref, plane_ref, anchor_ref, table, ordered, send1, recv1, right, grid_out, grid_in, send2, recv2, left, part_out, part_in, last_out, last_in,
    load_sems, table_sem, send_sems, recv_sems, grid_sems, part_sems, last_sems,
):
    me = lax.axis_index("facet")
    band = lax.axis_index("freq")
    my_share, my_column = me // RADIX, me % RADIX
    my_z, my_y = my_share // 4, my_share % 4
    special = jnp.where(my_y == 0, 1, 0)
    my_x, my_core = my_column // 2, my_column % 2
    rows = vis_ref.shape[1]
    cells = PLANES * SUB
    band_rows = TROWS // bands
    kept = KS // bands
    band_up = {"freq": lax.rem(band + 1, bands)}
    band_down = {"freq": lax.rem(band + bands - 1, bands)}

    pairs = (
        (vis_hbm, vis_ref), (target_hbm, target_ref), (cell_hbm, cell_ref), (plane_hbm, plane_ref),
        (anchor_hbm, anchor_ref),
    )
    loads = [pltpu.make_async_copy(*pair, load_sems.at[number]) for number, pair in enumerate(pairs)]
    for load in loads:
        load.start()
    load_table = pltpu.make_async_copy(table_hbm, table, table_sem)
    load_table.start()

    barrier = pltpu.get_barrier_semaphore()


    def column_at(x, c):
        return lax.rem(my_x + x, 4) * 2 + lax.rem(my_core + c, 2)

    def facet_at(z, y, x, c):
        return (lax.rem(my_z + z, 2) * 4 + lax.rem(my_y + y, 4)) * RADIX + column_at(x, c)

    for place in PLACES:
        pl.semaphore_signal(barrier, inc=1, device_id={"facet": facet_at(*place)}, device_id_type=MESH)

    pl.semaphore_signal(barrier, inc=1, device_id=band_up, device_id_type=MESH)
    pl.semaphore_signal(barrier, inc=1, device_id=band_down, device_id_type=MESH)

    for load in loads:
        load.wait()

    named = iota((facets, rows), 0) == target_ref[...]
    named_f = jnp.where(named, 1.0, 0.0)
    named_b = named_f.astype(BF16)
    earlier = jnp.where(iota((rows, rows), 0) < iota((rows, rows), 1), 1.0, 0.0).astype(BF16)
    position = jnp.sum(named_f * dot(named_b, earlier), axis=0, keepdims=True)
    here = iota((CAP, rows), 0).astype(F32) == position
    vis = vis_ref[...].astype(F32)
    cell = cell_ref[...]
    payloads = (
        vis[0:1], vis[1:2], (cell >> 8).astype(F32), (cell & 255).astype(F32), plane_ref[...].astype(F32),
    )
    spread = [jnp.where(here, payload, 0.0) for payload in payloads]
    spread.append(jnp.zeros((LANES - CAP * len(payloads), rows), F32))
    slots = nt_dot(named_b, jnp.concatenate(spread, axis=0).astype(BF16))
    lane = iota((facets, LANES), 1)
    us, vs = anchor_ref[0, 0], anchor_ref[0, 1]
    slots = jnp.where(lane == CAP * 5, us.astype(F32), slots)
    send1[...] = slots.reshape(facets, 1, LANES)
    recv1[pl.ds(me, 1)] = send1[pl.ds(me, 1)]

    pl.semaphore_wait(barrier, facets - 1 + 2)

    for place in PLACES:
        peer = facet_at(*place)
        send(send1.at[peer], recv1.at[me], send_sems.at[0], recv_sems.at[0], {"facet": peer})

    def settle(target, phase):
        return pltpu.make_async_remote_copy(
            src_ref=target.at[pl.ds(0, facets - 1)], dst_ref=target.at[pl.ds(0, facets - 1)],
            send_sem=send_sems.at[phase], recv_sem=recv_sems.at[phase],
            device_id={"facet": lax.rem(me + 1, facets)}, device_id_type=MESH,
        )

    low = iota((1, TCOLS), 1) < TCOLS // 2

    def swap(value):
        return pltpu.roll(value, TCOLS // 2, 1)

    for step in range(RADIX):
        group = column_at(*COLUMNS[step])
        spatial = vs + iota((SUB, TCOLS), 0)
        pixel = iota((SUB, TCOLS), 1)
        index = (((spatial & (RADIX - 1)) * group & (RADIX - 1)) << 13) + spatial * pixel
        cos_r, sin_r = turn(index)
        cos_s, sin_s = swap(cos_r), swap(sin_r)
        at = step * 2 * TCOLS
        right[:SUB, at:at + TCOLS] = jnp.where(low, cos_r, sin_s).astype(BF16)
        right[:SUB, at + TCOLS:at + 2 * TCOLS] = jnp.where(low, cos_s, sin_r).astype(BF16)
        right[SUB:, at:at + TCOLS] = jnp.where(low, -sin_r, cos_s).astype(BF16)
        right[SUB:, at + TCOLS:at + 2 * TCOLS] = jnp.where(low, -sin_s, cos_r).astype(BF16)

    load_table.wait()
    place = iota((SUB, SUB), 0)
    row_k = (((place >> 6) + band) & (bands - 1)) * kept + (place & (kept - 1))
    wanted = (row_k << 3) + ((((place >> 3) & (RADIX - 1)) - us) & (RADIX - 1))
    order = jnp.where(iota((SUB, SUB), 1) == wanted, 1.0, 0.0).astype(BF16)
    for part in range(2):
        ordered[part * SUB:(part + 1) * SUB] = nt_dot(order, table[part]).astype(BF16)

    wait1 = settle(recv1, 0)
    wait1.wait_recv()

    got = recv1[...].reshape(facets, LANES)
    every = iota((facets, cells), 1).astype(F32)
    v_cell = got[:, 3 * CAP:4 * CAP] + got[:, 4 * CAP:5 * CAP] * SUB
    b_parts = []
    for q0 in range(0, CAP, 4):
        pick_v = jnp.concatenate(
            [jnp.where(every == v_cell[:, q:q + 1], 1.0, 0.0).astype(BF16) for q in range(q0, q0 + 4)], axis=0
        )
        k_real = dot(pick_v, table[0])
        k_imag = dot(pick_v, table[1])
        v_real = jnp.concatenate([got[:, q:q + 1] for q in range(q0, q0 + 4)], axis=0)
        v_imag = jnp.concatenate([got[:, CAP + q:CAP + q + 1] for q in range(q0, q0 + 4)], axis=0)
        b_parts.append(
            ((v_real * k_real - v_imag * k_imag).astype(BF16), (v_real * k_imag + v_imag * k_real).astype(BF16))
        )
    b_real = jnp.concatenate([part[0] for part in b_parts], axis=0)
    b_imag = jnp.concatenate([part[1] for part in b_parts], axis=0)
    flat = got.T
    u_row = jnp.concatenate([flat[2 * CAP + q:2 * CAP + q + 1] for q in range(CAP)], axis=1)
    plane_row = jnp.concatenate([flat[4 * CAP + q:4 * CAP + q + 1] for q in range(CAP)], axis=1)
    pick_u = jnp.where(iota((SUB, facets * CAP), 0).astype(F32) == u_row, 1.0, 0.0).astype(BF16)
    pick_u = jnp.concatenate(
        [pick_u * jnp.where(plane_row == p, 1.0, 0.0).astype(BF16) for p in range(PLANES)], axis=0
    )
    a_both = dot(ordered[...], pick_u).astype(BF16)
    b_wide = jnp.concatenate([b_real, b_imag], axis=1)
    b_turned = jnp.concatenate([-b_imag, b_real], axis=1)
    quarter = SUB // bands
    gridded = dot(a_both[:SUB], b_wide) + dot(a_both[SUB:], b_turned)

    def grid_chunk(r, h):
        start = r * quarter + h * (quarter // 2)
        return gridded[start:start + quarter // 2]

    width = facets * 2 * kept
    own_s = iota((facets, width), 0) == (iota((facets, width), 1) >> 4)
    first = jnp.sum(jnp.where(own_s, got[:, 5 * CAP:5 * CAP + 1], 0.0), axis=0, keepdims=True).astype(I32)
    column = iota((1, width), 1)
    second = (column >> 3) & 1
    wanted = my_y + second * (RADIX - 2 * my_y)
    sign = 1 - 2 * second * (1 - special)
    fine = 32
    pieces = band_rows // fine
    coarse = iota((bands * pieces, width), 0)
    coarse = ((((coarse >> 3) + band) & (bands - 1)) << 3) + (coarse & (pieces - 1))

    def tables(residue, ahead):
        spatial = first + ((residue - first) & (RADIX - 1)) + (((column & (kept - 1)) + band * kept) << 3)
        spatial = (spatial * sign) & (NGRID - 1)
        return *turn(coarse * fine * spatial), *turn(iota((fine, width), 0) * spatial + ahead)

    def make_left():
        for piece in range(bands * pieces):
            block, at = piece // pieces, piece % pieces * fine
            c_r, c_i, f_r, f_i = tables_cos
            left[block, at:at + fine] = (c_r[piece:piece + 1] * f_r - c_i[piece:piece + 1] * f_i).astype(BF16)
            c_r, c_i, f_r, f_i = tables_sin
            left[block, band_rows + at:band_rows + at + fine] = (c_r[piece:piece + 1] * f_i + c_i[piece:piece + 1] * f_r).astype(BF16)

    ring = RingSum(grid_chunk, band_up, band_down, grid_out, grid_in, grid_sems.at[0], grid_sems.at[1])
    ring.start()
    ring.plain()
    tables_cos = tables(wanted, (special * second) << 14)
    tables_sin = tables(wanted + 4 * special, (special * (second + 1)) << 14)
    ring.middle()
    make_left()
    grid = ring.finish().astype(BF16)

    some = RADIX // 2
    conjugate = jnp.where(low, 1.0, -1.0)
    for part in range(2):
        span = some * 2 * TCOLS
        half = dot(grid, right[:, part * span:(part + 1) * span])
        for step in range(some):
            for z in range(2):
                at = (step * 2 + z) * TCOLS
                rows_of = [half[c * kept:(c + 1) * kept, at:at + TCOLS] for c in range(RADIX)]
                shares = [
                    (jnp.where(low, rows_of[0], swap(rows_of[4])), jnp.where(low, swap(rows_of[0]), rows_of[4])),
                    *((rows_of[c], rows_of[RADIX - c] * conjugate) for c in range(1, 4)),
                ]
                for y in range(4):
                    send2[part * some + step, z * 4 + y] = jnp.concatenate(shares[y], axis=0).astype(BF16)

        for place in PLACES:
            step = COLUMNS.index(place[2:])
            if step // some == part:
                peer = facet_at(*place)
                send(
                    send2.at[step, peer // RADIX], recv2.at[me], send_sems.at[1], recv_sems.at[1], {"facet": peer}
                )

    recv2[pl.ds(me, 1)] = send2[COLUMNS.index((0, 0)), pl.ds(my_share, 1)]

    wait2 = settle(recv2, 1)
    wait2.wait_recv()

    mixed = recv2[...].reshape(width, TCOLS)
    sections = part_out.shape[0]
    section_rows = band_rows // sections
    half_rows = section_rows // 2
    y_up, y_down = lax.rem(my_y + 1, 4), lax.rem(my_y + 3, 4)
    across = lax.rem(my_y + 2, 4)

    spec = special.astype(F32)
    below = jnp.where(low, 1.0, 0.0)
    plain = 1.0 - spec * (1.0 - below)
    kept_sine = spec * (1.0 - below)
    turned_sine = (1.0 - spec) * (1.0 - 2.0 * below)

    tiles = {}

    def tile_part(section, r, h):
        if r not in tiles:
            both = dot(left[r], mixed)
            cosines, sines = both[:band_rows], both[band_rows:]
            tiles[r] = cosines * plain + sines * kept_sine + swap(sines) * turned_sine
        at = section * section_rows + h * half_rows
        return tiles[r][at:at + half_rows]

    def phase(z, y):
        cos_c, sin_c = turn(jnp.zeros((1, TCOLS), I32) + ((my_y * (4 * z + y) & (RADIX - 1)) << 13))
        other = special * (1 - 2 * (y & 1))
        other = other.astype(F32) - sin_c
        return jnp.where(low, cos_c, other), jnp.where(low, other, cos_c)

    phases = {(z, n): phase(z, y) for z in range(2) for n, y in enumerate((my_y, y_up, across, y_down))}
    phases["pair"], phases["own"] = phase(1 - my_z, my_y), phase(my_z, my_y)

    class Last:
        def __init__(self, section, total):
            self.total, self.swapped = total, swap(total)
            self.out, self.came = last_out.at[section], last_in.at[section]
            self.send_sem, self.recv_sem = last_sems.at[0, section], last_sems.at[1, section]
            self.copies = []

        def turned(self, key):
            both = self.total * phases[key][0] + self.swapped * phases[key][1]
            return jnp.where(low, both[:half_rows], both[half_rows:])

        def go(self, out_slot, in_slot, value, z, y):
            self.out[out_slot] = value.astype(BF16)
            copy = send(
                self.out.at[out_slot], self.came.at[in_slot], self.send_sem.at[out_slot], self.recv_sem.at[in_slot],
                {"facet": (z * 4 + y) * RADIX + my_column},
            )
            self.copies.append(copy)

        def arrived(self, slot):
            pltpu.make_async_remote_copy(
                src_ref=self.out.at[slot], dst_ref=self.came.at[slot], send_sem=self.send_sem.at[slot],
                recv_sem=self.recv_sem.at[slot], device_id={"facet": lax.rem(me + 1, facets)}, device_id_type=MESH,
            ).wait_recv()
            return self.came[slot].astype(F32)

        def start(self):
            self.go(0, 0, self.turned((0, 2)), my_z, y_up)
            self.go(1, 1, self.turned((1, 2)), my_z, y_down)
            self.go(2, 2 + my_z, self.turned((1, 1)), 1, y_up)
            self.go(3, 4 + my_z, self.turned((0, 3)), 0, y_down)
            self.go(6, 6, self.turned("pair"), 1 - my_z, my_y)

        def middle(self):
            term_up, term_down = self.turned((0, 1)), self.turned((1, 3))
            self.go(4, 2 + my_z, term_up + self.arrived(0), 0, y_up)
            self.go(5, 4 + my_z, term_down + self.arrived(1), 1, y_down)

        def finish(self):
            came = [None, None, *(self.arrived(slot) for slot in range(2, 7))]
            own = self.turned("own")
            first = came[2] + came[4] + jnp.where(my_z == 0, own, came[6])
            other = came[3] + came[5] + jnp.where(my_z == 0, came[6], own)
            return jnp.concatenate(
                [jnp.where(low, first, swap(other)), jnp.where(low, swap(first), other)], axis=0
            )

    rings = [
        RingSum(
            functools.partial(tile_part, section), band_up, band_down,
            part_out.at[section], part_in.at[section], part_sems.at[0, section], part_sems.at[1, section],
        )
        for section in range(sections)
    ]
    for each in rings:
        each.start()
    for each in rings:
        each.plain()
    for each in rings:
        each.middle()
    lasts = []
    for section, each in enumerate(rings):
        lasts.append(Last(section, each.finish()))
        lasts[-1].start()
        if section:
            lasts[section - 1].middle()
    lasts[-1].middle()
    for section, each in enumerate(lasts):
        out_ref[section * section_rows:(section + 1) * section_rows] = each.finish() * scale

    for finished in [wait1, wait2]:
        finished.wait_send()
    for each in [ring, *rings, *lasts]:
        for copy in each.copies:
            copy.wait_send()


def shards(visibility, row_target, row_cell, row_plane, kernel_table, subgrid_anchor):
    facets = lax.axis_size("facet")
    bands = lax.axis_size("freq")
    rows = visibility.shape[2]
    scale = 1.0 / (SUB * math.sqrt(facets * bands * rows))
    kept = KS // bands
    band_rows = TROWS // bands
    vmem = pl.BlockSpec(memory_space=pltpu.VMEM)
    return pl.pallas_call(
        functools.partial(kernel, facets, bands, scale),
        out_shape=pltpu.VMEM((band_rows, TCOLS), F32),
        in_specs=[pl.BlockSpec(memory_space=pl.ANY)] * 6,
        out_specs=vmem,
        scratch_shapes=[
            pltpu.VMEM((2, rows), BF16),
            pltpu.VMEM((1, rows), I32),
            pltpu.VMEM((1, rows), I32),
            pltpu.VMEM((1, rows), I32),
            pltpu.SMEM((1, 2), I32),
            pltpu.VMEM((2, PLANES * SUB, SUB), BF16),
            pltpu.VMEM((2 * SUB, PLANES * SUB), BF16),
            pltpu.VMEM((facets, 1, LANES), F32),
            pltpu.VMEM((facets, 1, LANES), F32),
            pltpu.VMEM((2 * SUB, RADIX * 2 * TCOLS), BF16),
            pltpu.VMEM((6, SUB // bands // 2, 2 * SUB), BF16),
            pltpu.VMEM((6, SUB // bands // 2, 2 * SUB), BF16),
            pltpu.VMEM((RADIX, RADIX, 2 * kept, TCOLS), BF16),
            pltpu.VMEM((facets, 2 * kept, TCOLS), BF16),
            pltpu.VMEM((bands, 2 * band_rows, facets * 2 * kept), BF16),
            pltpu.VMEM((SECTIONS, 6, band_rows // SECTIONS // 2, TCOLS), BF16),
            pltpu.VMEM((SECTIONS, 6, band_rows // SECTIONS // 2, TCOLS), BF16),
            pltpu.VMEM((SECTIONS, 7, band_rows // SECTIONS // 2, TCOLS), BF16),
            pltpu.VMEM((SECTIONS, 7, band_rows // SECTIONS // 2, TCOLS), BF16),
            pltpu.SemaphoreType.DMA((5,)),
            pltpu.SemaphoreType.DMA,
            pltpu.SemaphoreType.DMA((2,)),
            pltpu.SemaphoreType.DMA((2,)),
            pltpu.SemaphoreType.DMA((2, 6)),
            pltpu.SemaphoreType.DMA((2, SECTIONS, 6)),
            pltpu.SemaphoreType.DMA((2, SECTIONS, 7)),
        ],
        compiler_params=pltpu.CompilerParams(
            collective_id=0, has_side_effects=True, vmem_limit_bytes=60 * 1024 * 1024
        ),
        cost_estimate=pl.CostEstimate(flops=8 * 10**9, bytes_accessed=4 * 10**6, transcendentals=0),
    )(
        visibility[0], row_target.reshape(1, rows), row_cell, row_plane, subgrid_anchor, kernel_table
    )


def solution(mesh):
    placed = (
        P("freq", None, "facet"),
        P("freq", "facet", None),
        P("freq", "facet"),
        P("freq", "facet"),
        P(),
        P("facet", None),
    )
    return jax.shard_map(
        shards, mesh=mesh, in_specs=placed, out_specs=P(("facet", "freq"), None), check_vma=False
    )
```

```python
import functools
import math

import jax
import jax.numpy as jnp
from jax import lax
from jax.experimental import pallas as pl
from jax.experimental.pallas import tpu as pltpu
from jax.sharding import PartitionSpec as P

NGRID = 65536
TROWS = 1024
TCOLS = 128
SUB = 256
PLANES = 8
CAP = 16
RADIX = 8
LANES = 128
KS = SUB // RADIX
SECTIONS = 2
PLACES = sorted(
    ((z, y, x, c) for z in range(2) for y in range(4) for x in range(4) for c in range(2) if z + y + x + c),
    key=lambda p: -(2 * p[0] + 2 * min(p[1], 4 - p[1]) + 2 * min(p[2], 4 - p[2]) + p[3]),
)
COLUMNS = tuple((x, c) for x in (2, 1, 3, 0) for c in (1, 0))
MESH = pl.DeviceIdType.MESH
F32, BF16, I32 = jnp.float32, jnp.bfloat16, jnp.int32


def turn(index):
    index = index & (NGRID - 1)
    quadrant = (index + NGRID // 8) >> 14
    rest = (index - (quadrant << 14)).astype(F32) * (2.0 * math.pi / NGRID)
    square = rest * rest
    sine = rest * (1.0 + square * (-1.0 / 6 + square * (1.0 / 120 + square * (-1.0 / 5040 + square * (1.0 / 362880)))))
    cosine = 1.0 + square * (-0.5 + square * (1.0 / 24 + square * (-1.0 / 720 + square * (1.0 / 40320))))
    odd = (quadrant & 1) == 1
    c = jnp.where(odd, sine, cosine)
    s = jnp.where(odd, cosine, sine)
    c = jnp.where(((quadrant + 1) & 2) == 2, -c, c)
    s = jnp.where((quadrant & 2) == 2, -s, s)
    return c, s


def iota(shape, dim):
    return lax.broadcasted_iota(I32, shape, dim)


def nt_dot(a, b):
    return lax.dot_general(a, b, (((1,), (1,)), ((), ())), preferred_element_type=F32)


def tn_dot(a, b):
    return lax.dot_general(a, b, (((0,), (0,)), ((), ())), preferred_element_type=F32)


def dot(a, b):
    return jnp.dot(a, b, preferred_element_type=F32)


def send(source, target, send_sem, recv_sem, device):
    copy = pltpu.make_async_remote_copy(
        src_ref=source, dst_ref=target, send_sem=send_sem, recv_sem=recv_sem,
        device_id=device, device_id_type=MESH,
    )
    copy.start()
    return copy


class RingSum:
    def __init__(self, chunk, up, down, out_ref, in_ref, send_sem, recv_sem):
        self.chunk, self.up, self.down = chunk, up, down
        self.out, self.came, self.send_sem, self.recv_sem = out_ref, in_ref, send_sem, recv_sem
        self.copies = []

    def go(self, slot, value, device):
        self.out[slot] = value.astype(BF16)
        copy = send(self.out.at[slot], self.came.at[slot], self.send_sem.at[slot], self.recv_sem.at[slot], device)
        self.copies.append(copy)

    def arrived(self, slot):
        self.copies[slot].wait_recv()
        return self.came[slot].astype(F32)

    def start(self):
        self.go(0, self.chunk(2, 0), self.up)
        self.go(1, self.chunk(2, 1), self.down)

    def plain(self):
        self.go(2, self.chunk(1, 1), self.up)
        self.go(3, self.chunk(3, 0), self.down)

    def middle(self):
        term_up, term_down = self.chunk(1, 0), self.chunk(3, 1)
        self.go(4, term_up + self.arrived(0), self.up)
        self.go(5, term_down + self.arrived(1), self.down)

    def finish(self):
        halves = [self.chunk(0, 0), self.chunk(0, 1)]
        halves = [halves[0] + self.arrived(3), halves[1] + self.arrived(2)]
        halves = [halves[0] + self.arrived(4), halves[1] + self.arrived(5)]
        return jnp.concatenate(halves, axis=0)


def kernel(
    facets, bands, scale,
    vis_hbm, target_hbm, cell_hbm, plane_hbm, anchor_hbm, table_hbm, out_ref,
    vis_ref, target_ref, cell_ref, plane_ref, anchor_ref, table, ordered, send1, recv1, right, grid_out, grid_in, send2, recv2, left, part_out, part_in, last_out, last_in,
    load_sems, table_sem, send_sems, recv_sems, grid_sems, part_sems, last_sems,
):
    me = lax.axis_index("facet")
    band = lax.axis_index("freq")
    my_share, my_column = me // RADIX, me % RADIX
    my_z, my_y = my_share // 4, my_share % 4
    special = jnp.where(my_y == 0, 1, 0)
    my_x, my_core = my_column // 2, my_column % 2
    rows = vis_ref.shape[1]
    cells = PLANES * SUB
    band_rows = TROWS // bands
    kept = KS // bands
    band_up = {"freq": lax.rem(band + 1, bands)}
    band_down = {"freq": lax.rem(band + bands - 1, bands)}

    pairs = (
        (vis_hbm, vis_ref), (target_hbm, target_ref), (cell_hbm, cell_ref), (plane_hbm, plane_ref),
        (anchor_hbm, anchor_ref),
    )
    loads = [pltpu.make_async_copy(*pair, load_sems.at[number]) for number, pair in enumerate(pairs)]
    for load in loads:
        load.start()
    load_table = pltpu.make_async_copy(table_hbm, table, table_sem)
    load_table.start()

    barrier = pltpu.get_barrier_semaphore()


    def column_at(x, c):
        return lax.rem(my_x + x, 4) * 2 + lax.rem(my_core + c, 2)

    def facet_at(z, y, x, c):
        return (lax.rem(my_z + z, 2) * 4 + lax.rem(my_y + y, 4)) * RADIX + column_at(x, c)

    for place in PLACES:
        pl.semaphore_signal(barrier, inc=1, device_id={"facet": facet_at(*place)}, device_id_type=MESH)

    pl.semaphore_signal(barrier, inc=1, device_id=band_up, device_id_type=MESH)
    pl.semaphore_signal(barrier, inc=1, device_id=band_down, device_id_type=MESH)

    for load in loads:
        load.wait()

    named = iota((facets, rows), 0) == target_ref[...]
    named_f = jnp.where(named, 1.0, 0.0)
    named_b = named_f.astype(BF16)
    earlier = jnp.where(iota((rows, rows), 0) < iota((rows, rows), 1), 1.0, 0.0).astype(BF16)
    position = jnp.sum(named_f * dot(named_b, earlier), axis=0, keepdims=True)
    here = iota((CAP, rows), 0).astype(F32) == position
    vis = vis_ref[...].astype(F32)
    cell = cell_ref[...]
    payloads = (
        vis[0:1], vis[1:2], (cell >> 8).astype(F32), (cell & 255).astype(F32), plane_ref[...].astype(F32),
    )
    spread = [jnp.where(here, payload, 0.0) for payload in payloads]
    spread.append(jnp.zeros((LANES - CAP * len(payloads), rows), F32))
    slots = nt_dot(named_b, jnp.concatenate(spread, axis=0).astype(BF16))
    lane = iota((facets, LANES), 1)
    us, vs = anchor_ref[0, 0], anchor_ref[0, 1]
    slots = jnp.where(lane == CAP * 5, us.astype(F32), slots)
    send1[...] = slots.reshape(facets, 1, LANES)
    recv1[pl.ds(me, 1)] = send1[pl.ds(me, 1)]

    pl.semaphore_wait(barrier, facets - 1 + 2)

    for place in PLACES:
        peer = facet_at(*place)
        send(send1.at[peer], recv1.at[me], send_sems.at[0], recv_sems.at[0], {"facet": peer})

    def settle(target, phase):
        return pltpu.make_async_remote_copy(
            src_ref=target.at[pl.ds(0, facets - 1)], dst_ref=target.at[pl.ds(0, facets - 1)],
            send_sem=send_sems.at[phase], recv_sem=recv_sems.at[phase],
            device_id={"facet": lax.rem(me + 1, facets)}, device_id_type=MESH,
        )

    low = iota((1, TCOLS), 1) < TCOLS // 2

    def swap(value):
        return pltpu.roll(value, TCOLS // 2, 1)

    for step in range(RADIX):
        group = column_at(*COLUMNS[step])
        spatial = vs + iota((SUB, TCOLS), 0)
        pixel = iota((SUB, TCOLS), 1)
        index = (((spatial & (RADIX - 1)) * group & (RADIX - 1)) << 13) + spatial * pixel
        cos_r, sin_r = turn(index)
        cos_s, sin_s = swap(cos_r), swap(sin_r)
        at = step * 2 * TCOLS
        right[:SUB, at:at + TCOLS] = jnp.where(low, cos_r, sin_s).astype(BF16)
        right[:SUB, at + TCOLS:at + 2 * TCOLS] = jnp.where(low, cos_s, sin_r).astype(BF16)
        right[SUB:, at:at + TCOLS] = jnp.where(low, -sin_r, cos_s).astype(BF16)
        right[SUB:, at + TCOLS:at + 2 * TCOLS] = jnp.where(low, -sin_s, cos_r).astype(BF16)

    load_table.wait()
    place = iota((SUB, SUB), 0)
    row_k = ((2 - (place >> 6) + band) & (bands - 1)) * kept + (place & (kept - 1))
    wanted = (row_k << 3) + ((((place >> 3) & (RADIX - 1)) - us) & (RADIX - 1))
    order = jnp.where(iota((SUB, SUB), 1) == wanted, 1.0, 0.0).astype(BF16)
    half_sub = SUB // 2
    for part in range(2):
        moved = nt_dot(order, table[part]).astype(BF16)
        for pair in range(2):
            ordered[pair, part * half_sub:(part + 1) * half_sub] = moved[pair * half_sub:(pair + 1) * half_sub]

    wait1 = settle(recv1, 0)
    wait1.wait_recv()

    got = recv1[...].reshape(facets, LANES)
    every = iota((facets, cells), 1).astype(F32)
    v_cell = got[:, 3 * CAP:4 * CAP] + got[:, 4 * CAP:5 * CAP] * SUB
    b_parts = []
    for q0 in range(0, CAP, 4):
        pick_v = jnp.concatenate(
            [jnp.where(every == v_cell[:, q:q + 1], 1.0, 0.0).astype(BF16) for q in range(q0, q0 + 4)], axis=0
        )
        k_real = dot(pick_v, table[0])
        k_imag = dot(pick_v, table[1])
        v_real = jnp.concatenate([got[:, q:q + 1] for q in range(q0, q0 + 4)], axis=0)
        v_imag = jnp.concatenate([got[:, CAP + q:CAP + q + 1] for q in range(q0, q0 + 4)], axis=0)
        b_parts.append(
            ((v_real * k_real - v_imag * k_imag).astype(BF16), (v_real * k_imag + v_imag * k_real).astype(BF16))
        )
    b_real = jnp.concatenate([part[0] for part in b_parts], axis=0)
    b_imag = jnp.concatenate([part[1] for part in b_parts], axis=0)
    flat = got.T
    u_row = jnp.concatenate([flat[2 * CAP + q:2 * CAP + q + 1] for q in range(CAP)], axis=1)
    plane_row = jnp.concatenate([flat[4 * CAP + q:4 * CAP + q + 1] for q in range(CAP)], axis=1)
    pick_u = jnp.where(iota((SUB, facets * CAP), 0).astype(F32) == u_row, 1.0, 0.0).astype(BF16)
    pick_u = jnp.concatenate(
        [pick_u * jnp.where(plane_row == p, 1.0, 0.0).astype(BF16) for p in range(PLANES)], axis=0
    )
    b_wide = jnp.concatenate([b_real, b_imag], axis=1)
    b_turned = jnp.concatenate([-b_imag, b_real], axis=1)
    quarter = SUB // bands
    made = {}

    def grid_chunk(r, h):
        pair, which = divmod((2 - r) % bands, 2)
        if pair not in made:
            a_pair = dot(ordered[pair], pick_u).astype(BF16)
            made[pair] = dot(a_pair[:half_sub], b_wide) + dot(a_pair[half_sub:], b_turned)
        start = which * quarter + h * (quarter // 2)
        return made[pair][start:start + quarter // 2]

    width = facets * 2 * kept
    own_s = iota((facets, width), 0) == (iota((facets, width), 1) >> 4)
    first = jnp.sum(jnp.where(own_s, got[:, 5 * CAP:5 * CAP + 1], 0.0), axis=0, keepdims=True).astype(I32)
    column = iota((1, width), 1)
    second = (column >> 3) & 1
    wanted = my_y + second * (RADIX - 2 * my_y)
    sign = 1 - 2 * second * (1 - special)
    fine = 32
    pieces = band_rows // fine
    coarse = iota((bands * pieces, width), 0)
    coarse = ((((coarse >> 3) + band) & (bands - 1)) << 3) + (coarse & (pieces - 1))

    def tables(residue, ahead):
        spatial = first + ((residue - first) & (RADIX - 1)) + (((column & (kept - 1)) + band * kept) << 3)
        spatial = (spatial * sign) & (NGRID - 1)
        return *turn(coarse * fine * spatial), *turn(iota((fine, width), 0) * spatial + ahead)

    def make_left():
        for piece in range(bands * pieces):
            block, at = piece // pieces, piece % pieces * fine
            c_r, c_i, f_r, f_i = tables_cos
            left[block, at:at + fine] = (c_r[piece:piece + 1] * f_r - c_i[piece:piece + 1] * f_i).astype(BF16)
            c_r, c_i, f_r, f_i = tables_sin
            left[block, band_rows + at:band_rows + at + fine] = (c_r[piece:piece + 1] * f_i + c_i[piece:piece + 1] * f_r).astype(BF16)

    ring = RingSum(grid_chunk, band_up, band_down, grid_out, grid_in, grid_sems.at[0], grid_sems.at[1])
    ring.start()
    ring.plain()
    tables_cos = tables(wanted, (special * second) << 14)
    tables_sin = tables(wanted + 4 * special, (special * (second + 1)) << 14)
    ring.middle()
    make_left()
    grid = ring.finish().astype(BF16)

    some = RADIX // 4
    conjugate = jnp.where(low, 1.0, -1.0)
    for part in range(4):
        span = some * 2 * TCOLS
        half = dot(grid, right[:, part * span:(part + 1) * span])
        for step in range(some):
            for z in range(2):
                at = (step * 2 + z) * TCOLS
                rows_of = [half[c * kept:(c + 1) * kept, at:at + TCOLS] for c in range(RADIX)]
                shares = [
                    (jnp.where(low, rows_of[0], swap(rows_of[4])), jnp.where(low, swap(rows_of[0]), rows_of[4])),
                    *((rows_of[c], rows_of[RADIX - c] * conjugate) for c in range(1, 4)),
                ]
                for y in range(4):
                    send2[part * some + step, z * 4 + y] = jnp.concatenate(shares[y], axis=0).astype(BF16)

        for place in PLACES:
            step = COLUMNS.index(place[2:])
            if step // some == part:
                peer = facet_at(*place)
                send(
                    send2.at[step, peer // RADIX], recv2.at[me], send_sems.at[1], recv_sems.at[1], {"facet": peer}
                )

    recv2[pl.ds(me, 1)] = send2[COLUMNS.index((0, 0)), pl.ds(my_share, 1)]

    wait2 = settle(recv2, 1)
    wait2.wait_recv()

    mixed = recv2[...].reshape(width, TCOLS)
    sections = part_out.shape[0]
    section_rows = band_rows // sections
    half_rows = section_rows // 2
    y_up, y_down = lax.rem(my_y + 1, 4), lax.rem(my_y + 3, 4)
    across = lax.rem(my_y + 2, 4)

    spec = special.astype(F32)
    below = jnp.where(low, 1.0, 0.0)
    plain = 1.0 - spec * (1.0 - below)
    kept_sine = spec * (1.0 - below)
    turned_sine = (1.0 - spec) * (1.0 - 2.0 * below)

    tiles = {}

    def tile_part(section, r, h):
        if r not in tiles:
            both = dot(left[r], mixed)
            cosines, sines = both[:band_rows], both[band_rows:]
            tiles[r] = cosines * plain + sines * kept_sine + swap(sines) * turned_sine
        at = section * section_rows + h * half_rows
        return tiles[r][at:at + half_rows]

    def phase(z, y):
        cos_c, sin_c = turn(jnp.zeros((1, TCOLS), I32) + ((my_y * (4 * z + y) & (RADIX - 1)) << 13))
        other = special * (1 - 2 * (y & 1))
        other = other.astype(F32) - sin_c
        return jnp.where(low, cos_c, other), jnp.where(low, other, cos_c)

    phases = {(z, n): phase(z, y) for z in range(2) for n, y in enumerate((my_y, y_up, across, y_down))}
    phases["pair"], phases["own"] = phase(1 - my_z, my_y), phase(my_z, my_y)

    class Last:
        def __init__(self, section, total):
            self.total, self.swapped = total, swap(total)
            self.out, self.came = last_out.at[section], last_in.at[section]
            self.send_sem, self.recv_sem = last_sems.at[0, section], last_sems.at[1, section]
            self.copies = []

        def turned(self, key):
            both = self.total * phases[key][0] + self.swapped * phases[key][1]
            return jnp.where(low, both[:half_rows], both[half_rows:])

        def go(self, out_slot, in_slot, value, z, y):
            self.out[out_slot] = value.astype(BF16)
            copy = send(
                self.out.at[out_slot], self.came.at[in_slot], self.send_sem.at[out_slot], self.recv_sem.at[in_slot],
                {"facet": (z * 4 + y) * RADIX + my_column},
            )
            self.copies.append(copy)

        def arrived(self, slot):
            pltpu.make_async_remote_copy(
                src_ref=self.out.at[slot], dst_ref=self.came.at[slot], send_sem=self.send_sem.at[slot],
                recv_sem=self.recv_sem.at[slot], device_id={"facet": lax.rem(me + 1, facets)}, device_id_type=MESH,
            ).wait_recv()
            return self.came[slot].astype(F32)

        def start(self):
            self.go(0, 0, self.turned((0, 2)), my_z, y_up)
            self.go(1, 1, self.turned((1, 2)), my_z, y_down)
            self.go(2, 2 + my_z, self.turned((1, 1)), 1, y_up)
            self.go(3, 4 + my_z, self.turned((0, 3)), 0, y_down)
            self.go(6, 6, self.turned("pair"), 1 - my_z, my_y)

        def middle(self):
            term_up, term_down = self.turned((0, 1)), self.turned((1, 3))
            self.go(4, 2 + my_z, term_up + self.arrived(0), 0, y_up)
            self.go(5, 4 + my_z, term_down + self.arrived(1), 1, y_down)

        def finish(self):
            came = [None, None, *(self.arrived(slot) for slot in range(2, 7))]
            own = self.turned("own")
            first = came[2] + came[4] + jnp.where(my_z == 0, own, came[6])
            other = came[3] + came[5] + jnp.where(my_z == 0, came[6], own)
            return jnp.concatenate(
                [jnp.where(low, first, swap(other)), jnp.where(low, swap(first), other)], axis=0
            )

    rings = [
        RingSum(
            functools.partial(tile_part, section), band_up, band_down,
            part_out.at[section], part_in.at[section], part_sems.at[0, section], part_sems.at[1, section],
        )
        for section in range(sections)
    ]
    for each in rings:
        each.start()
    for each in rings:
        each.plain()
    for each in rings:
        each.middle()
    lasts = []
    for section, each in enumerate(rings):
        lasts.append(Last(section, each.finish()))
        lasts[-1].start()
        if section:
            lasts[section - 1].middle()
    lasts[-1].middle()
    for section, each in enumerate(lasts):
        out_ref[section * section_rows:(section + 1) * section_rows] = each.finish() * scale

    for finished in [wait1, wait2]:
        finished.wait_send()
    for each in [ring, *rings, *lasts]:
        for copy in each.copies:
            copy.wait_send()


def shards(visibility, row_target, row_cell, row_plane, kernel_table, subgrid_anchor):
    facets = lax.axis_size("facet")
    bands = lax.axis_size("freq")
    rows = visibility.shape[2]
    scale = 1.0 / (SUB * math.sqrt(facets * bands * rows))
    kept = KS // bands
    band_rows = TROWS // bands
    vmem = pl.BlockSpec(memory_space=pltpu.VMEM)
    return pl.pallas_call(
        functools.partial(kernel, facets, bands, scale),
        out_shape=pltpu.VMEM((band_rows, TCOLS), F32),
        in_specs=[pl.BlockSpec(memory_space=pl.ANY)] * 6,
        out_specs=vmem,
        scratch_shapes=[
            pltpu.VMEM((2, rows), BF16),
            pltpu.VMEM((1, rows), I32),
            pltpu.VMEM((1, rows), I32),
            pltpu.VMEM((1, rows), I32),
            pltpu.SMEM((1, 2), I32),
            pltpu.VMEM((2, PLANES * SUB, SUB), BF16),
            pltpu.VMEM((2, SUB, PLANES * SUB), BF16),
            pltpu.VMEM((facets, 1, LANES), F32),
            pltpu.VMEM((facets, 1, LANES), F32),
            pltpu.VMEM((2 * SUB, RADIX * 2 * TCOLS), BF16),
            pltpu.VMEM((6, SUB // bands // 2, 2 * SUB), BF16),
            pltpu.VMEM((6, SUB // bands // 2, 2 * SUB), BF16),
            pltpu.VMEM((RADIX, RADIX, 2 * kept, TCOLS), BF16),
            pltpu.VMEM((facets, 2 * kept, TCOLS), BF16),
            pltpu.VMEM((bands, 2 * band_rows, facets * 2 * kept), BF16),
            pltpu.VMEM((SECTIONS, 6, band_rows // SECTIONS // 2, TCOLS), BF16),
            pltpu.VMEM((SECTIONS, 6, band_rows // SECTIONS // 2, TCOLS), BF16),
            pltpu.VMEM((SECTIONS, 7, band_rows // SECTIONS // 2, TCOLS), BF16),
            pltpu.VMEM((SECTIONS, 7, band_rows // SECTIONS // 2, TCOLS), BF16),
            pltpu.SemaphoreType.DMA((5,)),
            pltpu.SemaphoreType.DMA,
            pltpu.SemaphoreType.DMA((2,)),
            pltpu.SemaphoreType.DMA((2,)),
            pltpu.SemaphoreType.DMA((2, 6)),
            pltpu.SemaphoreType.DMA((2, SECTIONS, 6)),
            pltpu.SemaphoreType.DMA((2, SECTIONS, 7)),
        ],
        compiler_params=pltpu.CompilerParams(
            collective_id=0, has_side_effects=True, vmem_limit_bytes=60 * 1024 * 1024
        ),
        cost_estimate=pl.CostEstimate(flops=8 * 10**9, bytes_accessed=4 * 10**6, transcendentals=0),
    )(
        visibility[0], row_target.reshape(1, rows), row_cell, row_plane, subgrid_anchor, kernel_table
    )


def solution(mesh):
    placed = (
        P("freq", None, "facet"),
        P("freq", "facet", None),
        P("freq", "facet"),
        P("freq", "facet"),
        P(),
        P("facet", None),
    )
    return jax.shard_map(
        shards, mesh=mesh, in_specs=placed, out_specs=P(("facet", "freq"), None), check_vma=False
    )
```

```python
import functools
import math

import jax
import jax.numpy as jnp
from jax import lax
from jax.experimental import pallas as pl
from jax.experimental.pallas import tpu as pltpu
from jax.sharding import PartitionSpec as P

NGRID = 65536
TROWS = 1024
TCOLS = 128
SUB = 256
PLANES = 8
CAP = 16
RADIX = 8
LANES = 128
KS = SUB // RADIX
SECTIONS = 2
EARLY = 24
PLACES = sorted(
    ((z, y, x, c) for z in range(2) for y in range(4) for x in range(4) for c in range(2) if z + y + x + c),
    key=lambda p: -(2 * p[0] + 2 * min(p[1], 4 - p[1]) + 2 * min(p[2], 4 - p[2]) + p[3]),
)
COLUMNS = tuple((x, c) for x in (2, 1, 3, 0) for c in (1, 0))
MESH = pl.DeviceIdType.MESH
F32, BF16, I32 = jnp.float32, jnp.bfloat16, jnp.int32


def turn(index):
    index = index & (NGRID - 1)
    quadrant = (index + NGRID // 8) >> 14
    rest = (index - (quadrant << 14)).astype(F32) * (2.0 * math.pi / NGRID)
    square = rest * rest
    sine = rest * (1.0 + square * (-1.0 / 6 + square * (1.0 / 120 + square * (-1.0 / 5040 + square * (1.0 / 362880)))))
    cosine = 1.0 + square * (-0.5 + square * (1.0 / 24 + square * (-1.0 / 720 + square * (1.0 / 40320))))
    odd = (quadrant & 1) == 1
    c = jnp.where(odd, sine, cosine)
    s = jnp.where(odd, cosine, sine)
    c = jnp.where(((quadrant + 1) & 2) == 2, -c, c)
    s = jnp.where((quadrant & 2) == 2, -s, s)
    return c, s


def iota(shape, dim):
    return lax.broadcasted_iota(I32, shape, dim)


def nt_dot(a, b):
    return lax.dot_general(a, b, (((1,), (1,)), ((), ())), preferred_element_type=F32)


def tn_dot(a, b):
    return lax.dot_general(a, b, (((0,), (0,)), ((), ())), preferred_element_type=F32)


def dot(a, b):
    return jnp.dot(a, b, preferred_element_type=F32)


def send(source, target, send_sem, recv_sem, device):
    copy = pltpu.make_async_remote_copy(
        src_ref=source, dst_ref=target, send_sem=send_sem, recv_sem=recv_sem,
        device_id=device, device_id_type=MESH,
    )
    copy.start()
    return copy


class RingSum:
    def __init__(self, chunk, up, down, out_ref, in_ref, send_sem, recv_sem):
        self.chunk, self.up, self.down = chunk, up, down
        self.out, self.came, self.send_sem, self.recv_sem = out_ref, in_ref, send_sem, recv_sem
        self.copies = []

    def go(self, slot, value, device):
        self.out[slot] = value.astype(BF16)
        copy = send(self.out.at[slot], self.came.at[slot], self.send_sem.at[slot], self.recv_sem.at[slot], device)
        self.copies.append(copy)

    def arrived(self, slot):
        self.copies[slot].wait_recv()
        return self.came[slot].astype(F32)

    def start(self):
        self.go(0, self.chunk(2, 0), self.up)
        self.go(1, self.chunk(2, 1), self.down)

    def plain(self):
        self.go(2, self.chunk(1, 1), self.up)
        self.go(3, self.chunk(3, 0), self.down)

    def middle(self):
        term_up, term_down = self.chunk(1, 0), self.chunk(3, 1)
        self.go(4, term_up + self.arrived(0), self.up)
        self.go(5, term_down + self.arrived(1), self.down)

    def finish(self):
        halves = [self.chunk(0, 0), self.chunk(0, 1)]
        halves = [halves[0] + self.arrived(3), halves[1] + self.arrived(2)]
        halves = [halves[0] + self.arrived(4), halves[1] + self.arrived(5)]
        return jnp.concatenate(halves, axis=0)


def kernel(
    facets, bands, scale,
    vis_hbm, target_hbm, cell_hbm, plane_hbm, anchor_hbm, table_hbm, out_ref,
    vis_ref, target_ref, cell_ref, plane_ref, anchor_ref, table, ordered, send1, recv1, right, grid_out, grid_in, send2, recv2, left, part_out, part_in, last_out, last_in,
    load_sems, table_sem, send_sems, recv_sems, grid_sems, part_sems, last_sems,
):
    me = lax.axis_index("facet")
    band = lax.axis_index("freq")
    my_share, my_column = me // RADIX, me % RADIX
    my_z, my_y = my_share // 4, my_share % 4
    special = jnp.where(my_y == 0, 1, 0)
    my_x, my_core = my_column // 2, my_column % 2
    rows = vis_ref.shape[1]
    cells = PLANES * SUB
    band_rows = TROWS // bands
    kept = KS // bands
    band_up = {"freq": lax.rem(band + 1, bands)}
    band_down = {"freq": lax.rem(band + bands - 1, bands)}

    pairs = (
        (vis_hbm, vis_ref), (target_hbm, target_ref), (cell_hbm, cell_ref), (plane_hbm, plane_ref),
        (anchor_hbm, anchor_ref),
    )
    loads = [pltpu.make_async_copy(*pair, load_sems.at[number]) for number, pair in enumerate(pairs)]

    barrier = pltpu.get_barrier_semaphore()


    def column_at(x, c):
        return lax.rem(my_x + x, 4) * 2 + lax.rem(my_core + c, 2)

    def facet_at(z, y, x, c):
        return (lax.rem(my_z + z, 2) * 4 + lax.rem(my_y + y, 4)) * RADIX + column_at(x, c)

    for number, place in enumerate(PLACES):
        if number == EARLY:
            for load in loads:
                load.start()
        pl.semaphore_signal(barrier, inc=1, device_id={"facet": facet_at(*place)}, device_id_type=MESH)

    pl.semaphore_signal(barrier, inc=1, device_id=band_up, device_id_type=MESH)
    pl.semaphore_signal(barrier, inc=1, device_id=band_down, device_id_type=MESH)

    load_table = pltpu.make_async_copy(table_hbm, table, table_sem)
    load_table.start()
    for load in loads:
        load.wait()

    named = iota((facets, rows), 0) == target_ref[...]
    named_f = jnp.where(named, 1.0, 0.0)
    named_b = named_f.astype(BF16)
    earlier = jnp.where(iota((rows, rows), 0) < iota((rows, rows), 1), 1.0, 0.0).astype(BF16)
    position = jnp.sum(named_f * dot(named_b, earlier), axis=0, keepdims=True)
    here = iota((CAP, rows), 0).astype(F32) == position
    vis = vis_ref[...].astype(F32)
    cell = cell_ref[...]
    payloads = (
        vis[0:1], vis[1:2], (cell >> 8).astype(F32), (cell & 255).astype(F32), plane_ref[...].astype(F32),
    )
    spread = [jnp.where(here, payload, 0.0) for payload in payloads]
    spread.append(jnp.zeros((LANES - CAP * len(payloads), rows), F32))
    slots = nt_dot(named_b, jnp.concatenate(spread, axis=0).astype(BF16))
    lane = iota((facets, LANES), 1)
    us, vs = anchor_ref[0, 0], anchor_ref[0, 1]
    slots = jnp.where(lane == CAP * 5, us.astype(F32), slots)
    send1[...] = slots.reshape(facets, 1, LANES)
    recv1[pl.ds(me, 1)] = send1[pl.ds(me, 1)]

    pl.semaphore_wait(barrier, facets - 1 + 2)

    for place in PLACES:
        peer = facet_at(*place)
        send(send1.at[peer], recv1.at[me], send_sems.at[0], recv_sems.at[0], {"facet": peer})

    def settle(target, phase):
        return pltpu.make_async_remote_copy(
            src_ref=target.at[pl.ds(0, facets - 1)], dst_ref=target.at[pl.ds(0, facets - 1)],
            send_sem=send_sems.at[phase], recv_sem=recv_sems.at[phase],
            device_id={"facet": lax.rem(me + 1, facets)}, device_id_type=MESH,
        )

    low = iota((1, TCOLS), 1) < TCOLS // 2

    def swap(value):
        return pltpu.roll(value, TCOLS // 2, 1)

    for step in range(RADIX):
        group = column_at(*COLUMNS[step])
        spatial = vs + iota((SUB, TCOLS), 0)
        pixel = iota((SUB, TCOLS), 1)
        index = (((spatial & (RADIX - 1)) * group & (RADIX - 1)) << 13) + spatial * pixel
        cos_r, sin_r = turn(index)
        cos_s, sin_s = swap(cos_r), swap(sin_r)
        at = step * 2 * TCOLS
        right[:SUB, at:at + TCOLS] = jnp.where(low, cos_r, sin_s).astype(BF16)
        right[:SUB, at + TCOLS:at + 2 * TCOLS] = jnp.where(low, cos_s, sin_r).astype(BF16)
        right[SUB:, at:at + TCOLS] = jnp.where(low, -sin_r, cos_s).astype(BF16)
        right[SUB:, at + TCOLS:at + 2 * TCOLS] = jnp.where(low, -sin_s, cos_r).astype(BF16)

    load_table.wait()
    place = iota((SUB, SUB), 0)
    row_k = ((2 - (place >> 6) + band) & (bands - 1)) * kept + (place & (kept - 1))
    wanted = (row_k << 3) + ((((place >> 3) & (RADIX - 1)) - us) & (RADIX - 1))
    order = jnp.where(iota((SUB, SUB), 1) == wanted, 1.0, 0.0).astype(BF16)
    half_sub = SUB // 2
    for part in range(2):
        moved = nt_dot(order, table[part]).astype(BF16)
        for pair in range(2):
            ordered[pair, part * half_sub:(part + 1) * half_sub] = moved[pair * half_sub:(pair + 1) * half_sub]

    wait1 = settle(recv1, 0)
    wait1.wait_recv()

    got = recv1[...].reshape(facets, LANES)
    every = iota((facets, cells), 1).astype(F32)
    v_cell = got[:, 3 * CAP:4 * CAP] + got[:, 4 * CAP:5 * CAP] * SUB
    b_parts = []
    for q0 in range(0, CAP, 4):
        pick_v = jnp.concatenate(
            [jnp.where(every == v_cell[:, q:q + 1], 1.0, 0.0).astype(BF16) for q in range(q0, q0 + 4)], axis=0
        )
        k_real = dot(pick_v, table[0])
        k_imag = dot(pick_v, table[1])
        v_real = jnp.concatenate([got[:, q:q + 1] for q in range(q0, q0 + 4)], axis=0)
        v_imag = jnp.concatenate([got[:, CAP + q:CAP + q + 1] for q in range(q0, q0 + 4)], axis=0)
        b_parts.append(
            ((v_real * k_real - v_imag * k_imag).astype(BF16), (v_real * k_imag + v_imag * k_real).astype(BF16))
        )
    b_real = jnp.concatenate([part[0] for part in b_parts], axis=0)
    b_imag = jnp.concatenate([part[1] for part in b_parts], axis=0)
    flat = got.T
    u_row = jnp.concatenate([flat[2 * CAP + q:2 * CAP + q + 1] for q in range(CAP)], axis=1)
    plane_row = jnp.concatenate([flat[4 * CAP + q:4 * CAP + q + 1] for q in range(CAP)], axis=1)
    pick_u = jnp.where(iota((SUB, facets * CAP), 0).astype(F32) == u_row, 1.0, 0.0).astype(BF16)
    pick_u = jnp.concatenate(
        [pick_u * jnp.where(plane_row == p, 1.0, 0.0).astype(BF16) for p in range(PLANES)], axis=0
    )
    b_wide = jnp.concatenate([b_real, b_imag], axis=1)
    b_turned = jnp.concatenate([-b_imag, b_real], axis=1)
    quarter = SUB // bands
    made = {}

    def grid_chunk(r, h):
        pair, which = divmod((2 - r) % bands, 2)
        if pair not in made:
            a_pair = dot(ordered[pair], pick_u).astype(BF16)
            made[pair] = dot(a_pair[:half_sub], b_wide) + dot(a_pair[half_sub:], b_turned)
        start = which * quarter + h * (quarter // 2)
        return made[pair][start:start + quarter // 2]

    width = facets * 2 * kept
    own_s = iota((facets, width), 0) == (iota((facets, width), 1) >> 4)
    first = jnp.sum(jnp.where(own_s, got[:, 5 * CAP:5 * CAP + 1], 0.0), axis=0, keepdims=True).astype(I32)
    column = iota((1, width), 1)
    second = (column >> 3) & 1
    wanted = my_y + second * (RADIX - 2 * my_y)
    sign = 1 - 2 * second * (1 - special)
    fine = 32
    pieces = band_rows // fine
    coarse = iota((bands * pieces, width), 0)
    coarse = ((((coarse >> 3) + band) & (bands - 1)) << 3) + (coarse & (pieces - 1))

    def tables(residue, ahead):
        spatial = first + ((residue - first) & (RADIX - 1)) + (((column & (kept - 1)) + band * kept) << 3)
        spatial = (spatial * sign) & (NGRID - 1)
        return *turn(coarse * fine * spatial), *turn(iota((fine, width), 0) * spatial + ahead)

    def make_left():
        for piece in range(bands * pieces):
            block, at = piece // pieces, piece % pieces * fine
            c_r, c_i, f_r, f_i = tables_cos
            left[block, at:at + fine] = (c_r[piece:piece + 1] * f_r - c_i[piece:piece + 1] * f_i).astype(BF16)
            c_r, c_i, f_r, f_i = tables_sin
            left[block, band_rows + at:band_rows + at + fine] = (c_r[piece:piece + 1] * f_i + c_i[piece:piece + 1] * f_r).astype(BF16)

    ring = RingSum(grid_chunk, band_up, band_down, grid_out, grid_in, grid_sems.at[0], grid_sems.at[1])
    ring.start()
    ring.plain()
    tables_cos = tables(wanted, (special * second) << 14)
    tables_sin = tables(wanted + 4 * special, (special * (second + 1)) << 14)
    ring.middle()
    make_left()
    grid = ring.finish().astype(BF16)

    some = RADIX // 4
    conjugate = jnp.where(low, 1.0, -1.0)
    for part in range(4):
        span = some * 2 * TCOLS
        half = dot(grid, right[:, part * span:(part + 1) * span])
        for step in range(some):
            for z in range(2):
                at = (step * 2 + z) * TCOLS
                rows_of = [half[c * kept:(c + 1) * kept, at:at + TCOLS] for c in range(RADIX)]
                shares = [
                    (jnp.where(low, rows_of[0], swap(rows_of[4])), jnp.where(low, swap(rows_of[0]), rows_of[4])),
                    *((rows_of[c], rows_of[RADIX - c] * conjugate) for c in range(1, 4)),
                ]
                for y in range(4):
                    send2[part * some + step, z * 4 + y] = jnp.concatenate(shares[y], axis=0).astype(BF16)

        for place in PLACES:
            step = COLUMNS.index(place[2:])
            if step // some == part:
                peer = facet_at(*place)
                send(
                    send2.at[step, peer // RADIX], recv2.at[me], send_sems.at[1], recv_sems.at[1], {"facet": peer}
                )

    recv2[pl.ds(me, 1)] = send2[COLUMNS.index((0, 0)), pl.ds(my_share, 1)]

    wait2 = settle(recv2, 1)
    wait2.wait_recv()

    mixed = recv2[...].reshape(width, TCOLS)
    sections = part_out.shape[0]
    section_rows = band_rows // sections
    half_rows = section_rows // 2
    y_up, y_down = lax.rem(my_y + 1, 4), lax.rem(my_y + 3, 4)
    across = lax.rem(my_y + 2, 4)

    spec = special.astype(F32)
    below = jnp.where(low, 1.0, 0.0)
    plain = 1.0 - spec * (1.0 - below)
    kept_sine = spec * (1.0 - below)
    turned_sine = (1.0 - spec) * (1.0 - 2.0 * below)

    tiles = {}

    def tile_part(section, r, h):
        if r not in tiles:
            both = dot(left[r], mixed)
            cosines, sines = both[:band_rows], both[band_rows:]
            tiles[r] = cosines * plain + sines * kept_sine + swap(sines) * turned_sine
        at = section * section_rows + h * half_rows
        return tiles[r][at:at + half_rows]

    def phase(z, y):
        cos_c, sin_c = turn(jnp.zeros((1, TCOLS), I32) + ((my_y * (4 * z + y) & (RADIX - 1)) << 13))
        other = special * (1 - 2 * (y & 1))
        other = other.astype(F32) - sin_c
        return jnp.where(low, cos_c, other), jnp.where(low, other, cos_c)

    phases = {(z, n): phase(z, y) for z in range(2) for n, y in enumerate((my_y, y_up, across, y_down))}
    phases["pair"], phases["own"] = phase(1 - my_z, my_y), phase(my_z, my_y)

    class Last:
        def __init__(self, section, total):
            self.total, self.swapped = total, swap(total)
            self.out, self.came = last_out.at[section], last_in.at[section]
            self.send_sem, self.recv_sem = last_sems.at[0, section], last_sems.at[1, section]
            self.copies = []

        def turned(self, key):
            both = self.total * phases[key][0] + self.swapped * phases[key][1]
            return jnp.where(low, both[:half_rows], both[half_rows:])

        def go(self, out_slot, in_slot, value, z, y):
            self.out[out_slot] = value.astype(BF16)
            copy = send(
                self.out.at[out_slot], self.came.at[in_slot], self.send_sem.at[out_slot], self.recv_sem.at[in_slot],
                {"facet": (z * 4 + y) * RADIX + my_column},
            )
            self.copies.append(copy)

        def arrived(self, slot):
            pltpu.make_async_remote_copy(
                src_ref=self.out.at[slot], dst_ref=self.came.at[slot], send_sem=self.send_sem.at[slot],
                recv_sem=self.recv_sem.at[slot], device_id={"facet": lax.rem(me + 1, facets)}, device_id_type=MESH,
            ).wait_recv()
            return self.came[slot].astype(F32)

        def start(self):
            self.go(0, 0, self.turned((0, 2)), my_z, y_up)
            self.go(1, 1, self.turned((1, 2)), my_z, y_down)
            self.go(2, 2 + my_z, self.turned((1, 1)), 1, y_up)
            self.go(3, 4 + my_z, self.turned((0, 3)), 0, y_down)
            self.go(6, 6, self.turned("pair"), 1 - my_z, my_y)

        def middle(self):
            term_up, term_down = self.turned((0, 1)), self.turned((1, 3))
            self.go(4, 2 + my_z, term_up + self.arrived(0), 0, y_up)
            self.go(5, 4 + my_z, term_down + self.arrived(1), 1, y_down)

        def finish(self):
            came = [None, None, *(self.arrived(slot) for slot in range(2, 7))]
            own = self.turned("own")
            first = came[2] + came[4] + jnp.where(my_z == 0, own, came[6])
            other = came[3] + came[5] + jnp.where(my_z == 0, came[6], own)
            return jnp.concatenate(
                [jnp.where(low, first, swap(other)), jnp.where(low, swap(first), other)], axis=0
            )

    rings = [
        RingSum(
            functools.partial(tile_part, section), band_up, band_down,
            part_out.at[section], part_in.at[section], part_sems.at[0, section], part_sems.at[1, section],
        )
        for section in range(sections)
    ]
    for each in rings:
        each.start()
    for each in rings:
        each.plain()
    for each in rings:
        each.middle()
    lasts = []
    for section, each in enumerate(rings):
        lasts.append(Last(section, each.finish()))
        lasts[-1].start()
        if section:
            lasts[section - 1].middle()
    lasts[-1].middle()
    for section, each in enumerate(lasts):
        out_ref[section * section_rows:(section + 1) * section_rows] = each.finish() * scale

    for finished in [wait1, wait2]:
        finished.wait_send()
    for each in [ring, *rings, *lasts]:
        for copy in each.copies:
            copy.wait_send()


def shards(visibility, row_target, row_cell, row_plane, kernel_table, subgrid_anchor):
    facets = lax.axis_size("facet")
    bands = lax.axis_size("freq")
    rows = visibility.shape[2]
    scale = 1.0 / (SUB * math.sqrt(facets * bands * rows))
    kept = KS // bands
    band_rows = TROWS // bands
    vmem = pl.BlockSpec(memory_space=pltpu.VMEM)
    return pl.pallas_call(
        functools.partial(kernel, facets, bands, scale),
        out_shape=pltpu.VMEM((band_rows, TCOLS), F32),
        in_specs=[pl.BlockSpec(memory_space=pl.ANY)] * 6,
        out_specs=vmem,
        scratch_shapes=[
            pltpu.VMEM((2, rows), BF16),
            pltpu.VMEM((1, rows), I32),
            pltpu.VMEM((1, rows), I32),
            pltpu.VMEM((1, rows), I32),
            pltpu.SMEM((1, 2), I32),
            pltpu.VMEM((2, PLANES * SUB, SUB), BF16),
            pltpu.VMEM((2, SUB, PLANES * SUB), BF16),
            pltpu.VMEM((facets, 1, LANES), F32),
            pltpu.VMEM((facets, 1, LANES), F32),
            pltpu.VMEM((2 * SUB, RADIX * 2 * TCOLS), BF16),
            pltpu.VMEM((6, SUB // bands // 2, 2 * SUB), BF16),
            pltpu.VMEM((6, SUB // bands // 2, 2 * SUB), BF16),
            pltpu.VMEM((RADIX, RADIX, 2 * kept, TCOLS), BF16),
            pltpu.VMEM((facets, 2 * kept, TCOLS), BF16),
            pltpu.VMEM((bands, 2 * band_rows, facets * 2 * kept), BF16),
            pltpu.VMEM((SECTIONS, 6, band_rows // SECTIONS // 2, TCOLS), BF16),
            pltpu.VMEM((SECTIONS, 6, band_rows // SECTIONS // 2, TCOLS), BF16),
            pltpu.VMEM((SECTIONS, 7, band_rows // SECTIONS // 2, TCOLS), BF16),
            pltpu.VMEM((SECTIONS, 7, band_rows // SECTIONS // 2, TCOLS), BF16),
            pltpu.SemaphoreType.DMA((5,)),
            pltpu.SemaphoreType.DMA,
            pltpu.SemaphoreType.DMA((2,)),
            pltpu.SemaphoreType.DMA((2,)),
            pltpu.SemaphoreType.DMA((2, 6)),
            pltpu.SemaphoreType.DMA((2, SECTIONS, 6)),
            pltpu.SemaphoreType.DMA((2, SECTIONS, 7)),
        ],
        compiler_params=pltpu.CompilerParams(
            collective_id=0, has_side_effects=True, vmem_limit_bytes=60 * 1024 * 1024
        ),
        cost_estimate=pl.CostEstimate(flops=8 * 10**9, bytes_accessed=4 * 10**6, transcendentals=0),
    )(
        visibility[0], row_target.reshape(1, rows), row_cell, row_plane, subgrid_anchor, kernel_table
    )


def solution(mesh):
    placed = (
        P("freq", None, "facet"),
        P("freq", "facet", None),
        P("freq", "facet"),
        P("freq", "facet"),
        P(),
        P("facet", None),
    )
    return jax.shard_map(
        shards, mesh=mesh, in_specs=placed, out_specs=P(("facet", "freq"), None), check_vma=False
    )
```
